32 devices in a mesh: dp: 4 (over z), ctx: 2 (over x), head: 4 (over y, core).
Axes of the slice: x: 2, y: 2, z: 4, core: 2. Of those that a mesh axis runs over, the one named last changes fastest.
Arguments:
- queries: bfloat16 [4, 256, 64, 288], P('dp', 'ctx', 'head'), may hold values from -100 to 100
- latents: bfloat16 [4, 256, 288], P('dp', 'ctx'), may hold values from -16 to 16
- positions: int32 [4, 256], P('dp', 'ctx'), may hold values from 0 to 255, as said below
- lse: float32 [4, 256, 64], P('dp', 'ctx', 'head'), as said below
- saved_out: bfloat16 [4, 256, 64, 256], P('dp', 'ctx', 'head'), may hold values from -6 to 6
- out_grad: bfloat16 [4, 256, 64, 128], P('dp', 'ctx', 'head'), may hold values from -6 to 6
- value_up: bfloat16 [64, 256, 128], P('head'), may hold values from -0.375 to 0.375
Outputs:
- query_grad: bfloat16 [4, 256, 64, 288], P('dp', 'ctx', 'head')
- latent_grad: float32 [4, 256, 288], P('dp', 'ctx')
- value_up_grad: float32 [256, 64, 128], P(('dp', 'ctx'), 'head')
The draws below stay inside these ranges and needn't reach their ends.
Inputs may be any that keep to these rules, and one draw needn't show every extreme that they name: For each sequence the 256 positions are a permutation of 0 to 255; the 128 slots of each aligned block of 128 slots hold 128 consecutive positions, beginning at a multiple of 128, in some order. lse[b, i, h] is the logarithm of the sum over the slots j visible to i of exp(logits[i, j]).
All inputs are finite; a program needn't handle non-finite values.
Results may differ from the reference program's by a relative error of at most 0.014.
Values may be sent and summed in bfloat16 or wider, within the bound.
A program may use at most 64 MiB of HBM per device.

```python
import jax
import jax.numpy as jnp
from jax import lax

TOK_DEV = 128
HEADS = 64
LATENT = 256
ROPE = 32
VHEAD = 128
SLAB = 256
BATCH = 4


def draw_queries(key, part):
    key = jax.random.fold_in(key, 1)
    shape = (BATCH, SLAB, HEADS, LATENT + ROPE)
    values = jnp.clip(jax.random.normal(key, shape, jnp.float32), -6.0, 6.0)
    return values.astype(jnp.bfloat16)


def draw_latents(key, part):
    key = jax.random.fold_in(key, 2)
    shape = (BATCH, SLAB, LATENT + ROPE)
    values = jnp.clip(jax.random.normal(key, shape, jnp.float32), -6.0, 6.0)
    return values.astype(jnp.bfloat16)


def draw_positions(key, part):
    key = jax.random.fold_in(key, 3)
    block_count = SLAB // TOK_DEV
    first_key, second_key = jax.random.split(key)
    order = jax.vmap(lambda inner: jax.random.permutation(inner, block_count))(jax.random.split(first_key, BATCH))
    within = jax.vmap(lambda inner: jax.random.permutation(inner, TOK_DEV))(jax.random.split(second_key, BATCH * block_count))
    within = within.reshape(BATCH, block_count, TOK_DEV)
    return (order[:, :, None] * TOK_DEV + within).reshape(BATCH, SLAB).astype(jnp.int32)


def sequence_lse(query_rows, key_rows, key_pos):
    scaling = (VHEAD + ROPE) ** (-0.5)
    logits = jnp.dot(query_rows, key_rows.T, preferred_element_type=jnp.float32) * scaling
    visible = key_pos[None, :] <= key_pos[:, None]
    row_max = jnp.max(jnp.where(visible, logits, -1e+30), axis=-1)
    row_sum = jnp.sum(jnp.where(visible, jnp.exp(logits - row_max[:, None]), 0.0), axis=-1)
    return row_max + jnp.log(row_sum)


def draw_lse(key, part):
    queries = draw_queries(key, part)
    latents = draw_latents(key, part)
    positions = draw_positions(key, part)
    by_head = jnp.transpose(queries, (2, 0, 1, 3))

    def one_head(query_h):
        return jax.vmap(sequence_lse)(query_h, latents, positions)
    values = lax.map(one_head, by_head)
    return jnp.transpose(values, (1, 2, 0)).astype(jnp.float32)


def with_spikes(array, rng, source, target, shards_of, factor):
    owner, partner = [(jnp.arange(array.shape[axis_at]) // (array.shape[axis_at] // shards_of)).reshape([-1 if axis == axis_at else 1 for axis in range(array.ndim)]) for axis_at in (source, target)]
    chosen = jax.random.permutation(rng, shards_of)[partner]
    strong = (owner == chosen) | (owner == (partner + shards_of // 2) % shards_of)
    return jnp.where(strong, factor * array, array)


def level_of(key, extent, cuts, smallest, high):
    def one(dim, parts):
        draws = jax.random.uniform(jax.random.fold_in(jax.random.fold_in(key, 6), dim), (parts,), jnp.float32, smallest / len(cuts), high / len(cuts))
        return jnp.repeat(jnp.exp(draws), extent[dim] // parts).reshape((-1,) + (1,) * (len(extent) - dim - 1))

    loudness = one(*cuts[0])
    for cut in cuts[1:]:
        loudness = loudness * one(*cut)
    return loudness


def centred(rng, shape, spread, most, shards=(), held_as=jnp.bfloat16):
    entries = spread * jax.random.normal(rng, shape, jnp.float32)
    if shards:
        entries = entries * level_of(rng, shape, shards, -0.22, 0.18)
    return jnp.clip(entries, -most, most).astype(held_as)


def bell_draw_with(key, shape, spread, limit, cuts, heavy, held_as=jnp.bfloat16):
    result = spread * jax.random.normal(key, shape, jnp.float32)
    if cuts:
        result = result * level_of(key, shape, cuts, -0.22, 0.18)
    return jnp.clip(with_spikes(result, jax.random.fold_in(key, 3), *heavy), -limit, limit).astype(held_as)


def setup_inputs(seed: int = 0) -> dict:
    key_list = jax.random.split(jax.random.key(seed), 8)
    queries = draw_queries(jax.random.fold_in(key_list[7], 71), 0)
    latents = draw_latents(jax.random.fold_in(key_list[7], 71), 0)
    positions = draw_positions(jax.random.fold_in(key_list[7], 71), 0)
    lse = draw_lse(jax.random.fold_in(key_list[7], 71), 0)
    saved_out = bell_draw_with(key_list[4], (BATCH, SLAB, HEADS, LATENT), 1.0, 6.0, ((0, 4), (1, 2), (2, 4)), (1, 3, 2, 2.0))
    out_grad = centred(key_list[5], (BATCH, SLAB, HEADS, VHEAD), 1.0, 6.0, ((0, 4), (1, 2), (2, 4)))
    value_up = centred(key_list[6], (HEADS, LATENT, VHEAD), LATENT ** -0.5, 0.375, ((0, 4),))
    return {"queries": queries, "latents": latents, "positions": positions, "lse": lse, "saved_out": saved_out, "out_grad": out_grad, "value_up": value_up}


def head_grads(query_rows, grad_rows, saved_rows, up_matrix, key_rows, key_pos, lse_rows):
    latent_width = up_matrix.shape[0]
    scaling = (VHEAD + ROPE) ** -0.5
    logits = jnp.dot(query_rows, key_rows.T, preferred_element_type=jnp.float32) * scaling
    visible = key_pos[None, :] <= key_pos[:, None]
    lat_grad = jnp.dot(grad_rows, up_matrix.T, preferred_element_type=jnp.float32).astype(jnp.bfloat16)
    row_delta = jnp.sum(lat_grad.astype(jnp.float32) * saved_rows.astype(jnp.float32), axis=-1)
    weights = jnp.where(visible, jnp.exp(logits - lse_rows[:, None]), 0.0)
    dot_value = jnp.dot(lat_grad, key_rows[:, :latent_width].T, preferred_element_type=jnp.float32)
    dlogits = (weights * (dot_value - row_delta[:, None]) * scaling).astype(jnp.bfloat16)
    query_part = jnp.dot(dlogits, key_rows, preferred_element_type=jnp.float32).astype(jnp.bfloat16)
    key_part = jnp.dot(dlogits.T, query_rows, preferred_element_type=jnp.float32)
    value_part = jnp.dot(weights.astype(jnp.bfloat16).T, lat_grad, preferred_element_type=jnp.float32)
    rope_width = key_rows.shape[1] - latent_width
    key_part = key_part + jnp.pad(value_part, ((0, 0), (0, rope_width)))
    return query_part, key_part


def reference(queries, latents, positions, lse, saved_out, out_grad, value_up):
    def one_head(carry, head):
        query_h = lax.dynamic_index_in_dim(queries, head, 2, keepdims=False)
        grad_h = lax.dynamic_index_in_dim(out_grad, head, 2, keepdims=False)
        saved_h = lax.dynamic_index_in_dim(saved_out, head, 2, keepdims=False)
        lse_h = lax.dynamic_index_in_dim(lse, head, 2, keepdims=False)
        up_h = lax.dynamic_index_in_dim(value_up, head, 0, keepdims=False)
        query_part, key_part = jax.vmap(head_grads, in_axes=(0, 0, 0, None, 0, 0, 0))(
            query_h, grad_h, saved_h, up_h, latents, positions, lse_h)
        flat_saved = saved_h.reshape(-1, saved_h.shape[-1])
        flat_grad = grad_h.reshape(-1, grad_h.shape[-1])
        weight_part = jnp.dot(flat_saved.T, flat_grad, preferred_element_type=jnp.float32)
        return carry + key_part, (query_part, weight_part)

    start = jnp.zeros(latents.shape, jnp.float32)
    key_total, (query_parts, weight_parts) = lax.scan(one_head, start, jnp.arange(HEADS, dtype=jnp.int32))
    query_grad = jnp.transpose(query_parts, (1, 2, 0, 3))
    value_up_grad = jnp.transpose(weight_parts, (1, 0, 2))
    return query_grad, key_total, value_up_grad
```

```python
import functools

import jax
import jax.numpy as jnp
from jax import lax
from jax.experimental import pallas as pl
from jax.experimental.pallas import tpu as pltpu
from jax.sharding import PartitionSpec as P

ROPE = 32
VHEAD = 128
MESH = pl.DeviceIdType.MESH
BF16 = jnp.bfloat16
F32 = jnp.float32
CHUNKS = 4


def dot(lhs, rhs, over):
    return lax.dot_general(lhs, rhs, (((over[0],), (over[1],)), ((), ())), preferred_element_type=F32)


def kernel(
    dims,
    q_hbm, lat_hbm, pos_hbm, lse_hbm, saved_hbm, grad_hbm, up_hbm,
    qg_hbm, lg_out, vg_out,
    q_ref, kt_in, pos_in, lse_ref, saved_b, grad_b, up_ref,
    saved_lo, saved_hi, grad_f, saved_h, grad_h,
    keys, keys_t, bias,
    vx, vr, zs, zr,
    key_acc, ka_send, ka_recv, kb_send, kb_recv, kc,
    qg_ref,
    in_sem, lat_send, lat_recv, x_send, x_recv, z_send, z_recv,
    ka_ssem, ka_rsem, kb_sem, kc_ssem, kc_rsem, out_sem,
):
    n_dp, n_head, heads, slots, width, latent, share = dims
    scaling = (VHEAD + ROPE) ** -0.5
    my_dp, my_ctx, my_head = lax.axis_index("dp"), lax.axis_index("ctx"), lax.axis_index("head")
    other = 1 - my_ctx
    per_chunk = heads // CHUNKS
    piece = key_acc.shape[0] // n_head

    def load(index, source, target):
        copy = pltpu.make_async_copy(source, target, in_sem.at[index])
        copy.start()
        return copy

    lat_in = load(0, lat_hbm, kt_in.at[my_ctx])
    pos_load = load(1, pos_hbm, pos_in.at[my_ctx])
    saved_in = load(2, saved_hbm, saved_b)
    grad_in = load(3, grad_hbm, grad_b)
    up_in = load(4, up_hbm, up_ref)
    q_in = load(5, q_hbm, q_ref)
    lse_in = load(6, lse_hbm, lse_ref)

    barrier = pltpu.get_barrier_semaphore()
    pl.semaphore_signal(barrier, inc=1, device_id={"ctx": other}, device_id_type=MESH)
    for step in range(1, n_dp):
        pl.semaphore_signal(barrier, inc=1, device_id={"dp": lax.rem(my_dp + step, n_dp)}, device_id_type=MESH)
    for step in range(1, n_head):
        pl.semaphore_signal(barrier, inc=1, device_id={"head": lax.rem(my_head + step, n_head)}, device_id_type=MESH)
    lat_in.wait()
    pos_load.wait()
    pl.semaphore_wait(barrier, 1 + (n_dp - 1) + (n_head - 1))

    def send(source, target, send_sem, recv_sem, where):
        return pltpu.make_async_remote_copy(
            src_ref=source, dst_ref=target, send_sem=send_sem, recv_sem=recv_sem,
            device_id=where, device_id_type=MESH)

    lat_copy = send(kt_in.at[my_ctx], kt_in.at[my_ctx], lat_send.at[0], lat_recv.at[0], {"ctx": other})
    pos_copy = send(pos_in.at[my_ctx], pos_in.at[my_ctx], lat_send.at[1], lat_recv.at[1], {"ctx": other})
    lat_copy.start()
    pos_copy.start()

    saved_in.wait()
    grad_in.wait()
    rows_step = (slots * heads) // 8

    def widen(step, carry):
        rows = pl.ds(pl.multiple_of(step * rows_step, rows_step), rows_step)
        saved_lo[rows, :] = saved_b[rows, :128].astype(F32)
        saved_hi[rows, :] = saved_b[rows, 128:].astype(F32)
        grad_f[rows, :] = grad_b[rows, :].astype(F32)
        return carry

    lax.fori_loop(0, 8, widen, 0)

    def up_partial(head, carry):
        rows = pl.ds(head, slots, heads)
        low = saved_lo[rows, :].astype(BF16)
        high = saved_hi[rows, :].astype(BF16)
        grad = grad_f[rows, :].astype(BF16)
        saved_h[head, :, :128] = low
        saved_h[head, :, 128:] = high
        grad_h[head] = grad
        product = jnp.concatenate([dot(low, grad, (0, 0)), dot(high, grad, (0, 0))], axis=0).astype(BF16)
        for dp in range(n_dp):
            for ctx in range(2):
                first = (dp * 2 + ctx) * share
                vx[ctx, head, dp] = product[first:first + share]
        return carry

    x_copies = []
    for chunk in range(CHUNKS):
        lax.fori_loop(chunk * per_chunk, (chunk + 1) * per_chunk, up_partial, 0)
        part = pl.ds(chunk * per_chunk, per_chunk)
        copy = send(vx.at[other, part], vr.at[part], x_send.at[chunk], x_recv.at[chunk], {"ctx": other})
        copy.start()
        x_copies.append(copy)

    lat_copy.wait_recv()
    pos_copy.wait_recv()
    query_pos = pos_in[my_ctx]
    for half in range(2):
        cols = slice(half * slots, (half + 1) * slots)
        block = kt_in[half]
        keys_t[:, cols] = block
        keys[cols, :] = block.astype(F32).T.astype(BF16)
        key_pos = jnp.broadcast_to(pos_in[half], (slots, slots)).T
        bias[cols, :] = jnp.where(key_pos <= query_pos, 0.0, -1e30)
    key_acc[...] = jnp.zeros_like(key_acc)
    up_in.wait()
    q_in.wait()
    lse_in.wait()
    diagonal = lax.broadcasted_iota(jnp.int32, (slots, slots), 0) == lax.broadcasted_iota(
        jnp.int32, (slots, slots), 1)

    def attend(pair, carry):
        one, two = 2 * pair, 2 * pair + 1
        lat_grads, deltas = [], []
        for head in (one, two):
            lat_grad = dot(up_ref[head], grad_h[head], (1, 1)).astype(BF16)
            lat_grads.append(lat_grad)
            full = dot(saved_h[head], lat_grad, (1, 0))
            deltas.append(jnp.sum(jnp.where(diagonal, full, 0.0), axis=0, keepdims=True))
        lat_grad = jnp.concatenate(lat_grads, axis=1)
        delta = jnp.concatenate(deltas, axis=1)
        query = jnp.concatenate([q_ref[one], q_ref[two]], axis=1)
        lse = jnp.concatenate([lse_ref[pl.ds(one, 1), :], lse_ref[pl.ds(two, 1), :]], axis=1)
        mask = jnp.concatenate([bias[...], bias[...]], axis=1)
        logits = dot(keys[...], query, (1, 0)) * scaling
        weights = jnp.exp(logits - lse + mask)
        dot_value = dot(keys[:, :latent], lat_grad, (1, 0))
        dlogits = (weights * (dot_value - delta) * scaling).astype(BF16)
        weights_b = weights.astype(BF16)
        query_grad = dot(keys_t[...], dlogits, (1, 0)).astype(BF16)
        qg_ref[one] = query_grad[:, :slots]
        qg_ref[two] = query_grad[:, slots:]
        key_term = dot(query, dlogits, (1, 1))
        value_term = dot(lat_grad, weights_b, (1, 1))
        key_acc[:latent, :] += key_term[:latent] + value_term
        key_acc[latent:width, :] += key_term[latent:]
        return carry

    z_copies = []

    def forward(chunk):
        x_copies[chunk].wait_recv()

        def add(head, carry):
            for dp in range(n_dp):
                zs[dp, head] = (vx[my_ctx, head, dp].astype(F32) + vr[head, dp].astype(F32)).astype(BF16)
            return carry

        lax.fori_loop(chunk * per_chunk, (chunk + 1) * per_chunk, add, 0)
        part = pl.ds(chunk * per_chunk, per_chunk)
        for step in range(1, n_dp):
            to = lax.rem(my_dp + step, n_dp)
            copy = send(zs.at[to, part], zr.at[my_dp, part], z_send.at[to, chunk], z_recv.at[my_dp, chunk], {"dp": to})
            copy.start()
            z_copies.append(copy)

    def attend_chunk(chunk):
        lax.fori_loop(chunk * per_chunk // 2, (chunk + 1) * per_chunk // 2, attend, 0)

    attend_chunk(0)
    attend_chunk(1)
    forward(0)
    attend_chunk(2)
    attend_chunk(3)
    qg_copy = pltpu.make_async_copy(qg_ref, qg_hbm, out_sem)
    qg_copy.start()

    for part in range(n_head):
        for ctx in range(2):
            ka_send[part, ctx] = key_acc[
                part * piece:(part + 1) * piece, ctx * slots:(ctx + 1) * slots].astype(BF16)
    ka_copies = []
    for step in range(1, n_head):
        to = lax.rem(my_head + step, n_head)
        copy = send(ka_send.at[to], ka_recv.at[my_head], ka_ssem.at[to], ka_rsem.at[my_head], {"head": to})
        copy.start()
        ka_copies.append(copy)

    forward(1)

    sums = ka_send[my_head].astype(F32)
    for step in range(1, n_head):
        src = lax.rem(my_head + step, n_head)
        send(ka_send.at[src], ka_recv.at[src], ka_ssem.at[src], ka_rsem.at[src], {"head": src}).wait_recv()
        sums = sums + ka_recv[src].astype(F32)
    kb_send[...] = sums.astype(BF16)
    kb_copy = send(kb_send.at[other], kb_recv, kb_sem.at[0], kb_sem.at[1], {"ctx": other})
    kb_copy.start()

    forward(2)

    kb_copy.wait_recv()
    kc[my_head] = (kb_send[my_ctx].astype(F32) + kb_recv[...].astype(F32)).astype(BF16)
    kc_copies = []
    for step in range(1, n_head):
        to = lax.rem(my_head + step, n_head)
        copy = send(kc.at[my_head], kc.at[my_head], kc_ssem.at[to], kc_rsem.at[my_head], {"head": to})
        copy.start()
        kc_copies.append(copy)

    forward(3)

    for step in range(1, n_head):
        src = lax.rem(my_head + step, n_head)
        send(kc.at[src], kc.at[src], kc_ssem.at[src], kc_rsem.at[src], {"head": src}).wait_recv()
    for part in range(n_head):
        first, last = part * piece, min((part + 1) * piece, width)
        lg_out[first:last, :] = kc[part, :last - first, :].astype(F32)

    def finish(head, carry):
        total = zs[my_dp, head].astype(F32)
        for step in range(1, n_dp):
            total = total + zr[lax.rem(my_dp + step, n_dp), head].astype(F32)
        vg_out[pl.ds(head, share, heads), :] = total
        return carry

    for chunk in range(CHUNKS):
        part = pl.ds(chunk * per_chunk, per_chunk)
        for step in range(1, n_dp):
            src = lax.rem(my_dp + step, n_dp)
            send(zs.at[src, part], zr.at[src, part], z_send.at[src, chunk], z_recv.at[src, chunk],
                 {"dp": src}).wait_recv()
        lax.fori_loop(chunk * per_chunk, (chunk + 1) * per_chunk, finish, 0)

    for copy in [lat_copy, pos_copy, kb_copy] + x_copies + z_copies + ka_copies + kc_copies:
        copy.wait_send()
    qg_copy.wait()


def fused(mesh, queries, latents, positions, lse, saved_out, out_grad, value_up):
    n_dp, n_head = mesh.shape["dp"], mesh.shape["head"]
    _, slots, heads, width = queries.shape
    latent = saved_out.shape[3]
    vhead = out_grad.shape[3]
    share = latent // (n_dp * 2)
    unit = 16 * n_head
    piece = -(-width // unit) * 16
    dims = (n_dp, n_head, heads, slots, width, latent, share)
    dma = pltpu.SemaphoreType.DMA
    query_grad, latent_grad, up_grad = pl.pallas_call(
        functools.partial(kernel, dims),
        out_shape=(
            jax.ShapeDtypeStruct((heads, width, slots), BF16),
            jax.ShapeDtypeStruct((width, slots), F32),
            jax.ShapeDtypeStruct((share * heads, vhead), F32),
        ),
        in_specs=[pl.BlockSpec(memory_space=pl.ANY)] * 7,
        out_specs=(
            pl.BlockSpec(memory_space=pl.ANY),
            pl.BlockSpec(memory_space=pltpu.VMEM),
            pl.BlockSpec(memory_space=pltpu.VMEM),
        ),
        scratch_shapes=[
            pltpu.VMEM((heads, width, slots), BF16),
            pltpu.VMEM((2, width, slots), BF16),
            pltpu.VMEM((2, 1, slots), jnp.int32),
            pltpu.VMEM((heads, slots), F32),
            pltpu.VMEM((slots * heads, latent), BF16),
            pltpu.VMEM((slots * heads, vhead), BF16),
            pltpu.VMEM((heads, latent, vhead), BF16),
            pltpu.VMEM((slots * heads, 128), F32),
            pltpu.VMEM((slots * heads, 128), F32),
            pltpu.VMEM((slots * heads, vhead), F32),
            pltpu.VMEM((heads, slots, latent), BF16),
            pltpu.VMEM((heads, slots, vhead), BF16),
            pltpu.VMEM((2 * slots, width), BF16),
            pltpu.VMEM((width, 2 * slots), BF16),
            pltpu.VMEM((2 * slots, slots), F32),
            pltpu.VMEM((2, heads, n_dp, share, vhead), BF16),
            pltpu.VMEM((heads, n_dp, share, vhead), BF16),
            pltpu.VMEM((n_dp, heads, share, vhead), BF16),
            pltpu.VMEM((n_dp, heads, share, vhead), BF16),
            pltpu.VMEM((piece * n_head, 2 * slots), F32),
            pltpu.VMEM((n_head, 2, piece, slots), BF16),
            pltpu.VMEM((n_head, 2, piece, slots), BF16),
            pltpu.VMEM((2, piece, slots), BF16),
            pltpu.VMEM((piece, slots), BF16),
            pltpu.VMEM((n_head, piece, slots), BF16),
            pltpu.VMEM((heads, width, slots), BF16),
            dma((7,)),
            dma((2,)), dma((2,)),
            dma((CHUNKS,)), dma((CHUNKS,)),
            dma((n_dp, CHUNKS)), dma((n_dp, CHUNKS)),
            dma((n_head,)), dma((n_head,)),
            dma((2,)),
            dma((n_head,)), dma((n_head,)),
            dma,
        ],
        compiler_params=pltpu.CompilerParams(
            collective_id=0, has_side_effects=True, vmem_limit_bytes=48 * 1024 * 1024),
    )(
        jnp.transpose(queries[0], (1, 2, 0)),
        latents[0].T,
        positions,
        lse[0].T,
        saved_out.reshape(slots * heads, latent),
        out_grad.reshape(slots * heads, vhead),
        value_up,
    )
    return (
        jnp.transpose(query_grad, (2, 0, 1))[None],
        latent_grad.T[None],
        up_grad.reshape(share, heads, vhead),
    )


def spans(length):
    return [(lower, min(length, lower + 512)) for lower in range(0, length, 512)]


def spread(queries, latents, positions, lse, saved_out, out_grad, value_up):
    query_rows = queries[0]
    slot_count = query_rows.shape[0]
    head_count = query_rows.shape[1]
    full_width = query_rows.shape[2]
    latent_width = saved_out.shape[3]
    query_pos = positions[0]
    row_lse = lse[0]
    latest = jnp.max(query_pos)
    scaling = (VHEAD + ROPE) ** (-0.5)
    lat_grad = jnp.einsum(
        "thv,hlv->thl", out_grad[0], value_up, preferred_element_type=jnp.float32
    ).astype(jnp.bfloat16)
    row_delta = jnp.sum(lat_grad.astype(jnp.float32) * saved_out[0].astype(jnp.float32), axis=-1)
    slab_rows = slot_count * lax.axis_size("ctx")
    carry = (
        jnp.zeros((slot_count, head_count, full_width), jnp.float32),
        jnp.zeros((slab_rows, full_width), jnp.float32),
    )
    keys_in = lax.all_gather(latents[0], "ctx", axis=0, tiled=True)
    pos_in = lax.all_gather(positions[0], "ctx", axis=0, tiled=True)
    for lower, upper in spans(keys_in.shape[0]):
        key_rows = keys_in[lower:upper]
        key_pos = pos_in[lower:upper]

        def update(state):
            query_acc, key_acc = state
            logits = (
                jnp.einsum("thd,kd->thk", query_rows, key_rows, preferred_element_type=jnp.float32)
                * scaling
            )
            visible = key_pos[None, None, :] <= query_pos[:, None, None]
            weights = jnp.where(visible, jnp.exp(logits - row_lse[:, :, None]), 0.0)
            dot_value = jnp.einsum(
                "thl,kl->thk",
                lat_grad,
                key_rows[:, :latent_width],
                preferred_element_type=jnp.float32,
            )
            dlogits = (weights * (dot_value - row_delta[:, :, None]) * scaling).astype(jnp.bfloat16)
            query_acc = query_acc + jnp.einsum(
                "thk,kd->thd", dlogits, key_rows, preferred_element_type=jnp.float32
            )
            key_term = jnp.einsum(
                "thk,thd->kd", dlogits, query_rows, preferred_element_type=jnp.float32
            )
            value_term = jnp.einsum(
                "thk,thl->kl",
                weights.astype(jnp.bfloat16),
                lat_grad,
                preferred_element_type=jnp.float32,
            )
            key_term = key_term + jnp.pad(value_term, ((0, 0), (0, full_width - latent_width)))
            previous = lax.dynamic_slice_in_dim(key_acc, 0 + lower, upper - lower, 0)
            key_acc = lax.dynamic_update_slice_in_dim(key_acc, previous + key_term, 0 + lower, 0)
            return (query_acc, key_acc)

        carry = lax.cond(jnp.min(key_pos) > latest, lambda state: state, update, carry)
    query_acc, key_acc = carry
    summed = lax.psum(key_acc, "head")
    own_rows = lax.psum_scatter(summed, "ctx", scatter_dimension=0, tiled=True)
    weight_share = lax.psum_scatter(
        jnp.einsum("thl,thv->lhv", saved_out[0], out_grad[0], preferred_element_type=jnp.float32),
        ("dp", "ctx"),
        scatter_dimension=0,
        tiled=True,
    )
    return (query_acc.astype(jnp.bfloat16)[None], own_rows[None], weight_share)


def solution(mesh):
    body = functools.partial(fused, mesh) if mesh.shape["ctx"] == 2 else spread
    return jax.shard_map(
        body,
        mesh=mesh,
        in_specs=(
            P("dp", "ctx", "head", None),
            P("dp", "ctx", None),
            P("dp", "ctx"),
            P("dp", "ctx", "head"),
            P("dp", "ctx", "head", None),
            P("dp", "ctx", "head", None),
            P("head", None, None),
        ),
        out_specs=(
            P("dp", "ctx", "head", None),
            P("dp", "ctx", None),
            P(("dp", "ctx"), "head", None),
        ),
        check_vma=False,
    )
```

```python
import functools

import jax
import jax.numpy as jnp
from jax import lax
from jax.experimental import pallas as pl
from jax.experimental.pallas import tpu as pltpu
from jax.sharding import PartitionSpec as P

ROPE = 32
VHEAD = 128
MESH = pl.DeviceIdType.MESH
BF16 = jnp.bfloat16
F32 = jnp.float32
PER_CHUNK = 2


def dot(lhs, rhs, over):
    return lax.dot_general(lhs, rhs, (((over[0],), (over[1],)), ((), ())), preferred_element_type=F32)


def kernel(
    dims,
    q_hbm, lat_hbm, pos_hbm, lse_hbm, saved_hbm, grad_hbm, up_hbm,
    qg_hbm, lg_out, vg_out,
    q_ref, kt_in, pos_in, lse_ref, saved_b, grad_b, up_ref,
    saved_lo, saved_hi, grad_f, saved_h, grad_h,
    keys, keys_t, bias,
    vx, vr, zs, zr,
    key_acc, ka_send, ka_recv, kb_send, kb_recv, kc,
    qg_ref,
    in_sem, lat_send, lat_recv, x_send, x_recv, z_send, z_recv,
    ka_ssem, ka_rsem, kb_sem, kc_ssem, kc_rsem, out_sem,
):
    n_dp, n_head, heads, slots, width, latent, share = dims
    scaling = (VHEAD + ROPE) ** -0.5
    my_dp, my_ctx, my_head = lax.axis_index("dp"), lax.axis_index("ctx"), lax.axis_index("head")
    other = 1 - my_ctx
    chunks = heads // PER_CHUNK
    piece = key_acc.shape[0] // n_head

    def load(index, source, target):
        copy = pltpu.make_async_copy(source, target, in_sem.at[index])
        copy.start()
        return copy

    lat_in = load(0, lat_hbm, kt_in.at[my_ctx])
    pos_load = load(1, pos_hbm, pos_in.at[my_ctx])
    saved_in = load(2, saved_hbm, saved_b)
    grad_in = load(3, grad_hbm, grad_b)
    up_in = load(4, up_hbm, up_ref)
    q_in = load(5, q_hbm, q_ref)
    lse_in = load(6, lse_hbm, lse_ref)

    barrier = pltpu.get_barrier_semaphore()
    pl.semaphore_signal(barrier, inc=1, device_id={"ctx": other}, device_id_type=MESH)
    for step in range(1, n_dp):
        pl.semaphore_signal(barrier, inc=1, device_id={"dp": lax.rem(my_dp + step, n_dp)}, device_id_type=MESH)
    for step in range(1, n_head):
        pl.semaphore_signal(barrier, inc=1, device_id={"head": lax.rem(my_head + step, n_head)}, device_id_type=MESH)
    lat_in.wait()
    pos_load.wait()
    pl.semaphore_wait(barrier, 1 + (n_dp - 1) + (n_head - 1))

    def send(source, target, send_sem, recv_sem, where):
        return pltpu.make_async_remote_copy(
            src_ref=source, dst_ref=target, send_sem=send_sem, recv_sem=recv_sem,
            device_id=where, device_id_type=MESH)

    lat_copy = send(kt_in.at[my_ctx], kt_in.at[my_ctx], lat_send.at[0], lat_recv.at[0], {"ctx": other})
    pos_copy = send(pos_in.at[my_ctx], pos_in.at[my_ctx], lat_send.at[1], lat_recv.at[1], {"ctx": other})
    lat_copy.start()
    pos_copy.start()

    saved_in.wait()
    grad_in.wait()
    rows_step = (slots * heads) // 8

    def widen(step, carry):
        rows = pl.ds(pl.multiple_of(step * rows_step, rows_step), rows_step)
        saved_lo[rows, :] = saved_b[rows, :128].astype(F32)
        saved_hi[rows, :] = saved_b[rows, 128:].astype(F32)
        grad_f[rows, :] = grad_b[rows, :].astype(F32)
        return carry

    lax.fori_loop(0, 8, widen, 0)

    def x_copy(chunk):
        part = pl.ds(chunk * PER_CHUNK, PER_CHUNK)
        return send(vx.at[other, part], vr.at[part], x_send.at[chunk], x_recv.at[chunk], {"ctx": other})

    def up_partial(chunk, carry):
        for offset in range(PER_CHUNK):
            head = chunk * PER_CHUNK + offset
            rows = pl.ds(head, slots, heads)
            low = saved_lo[rows, :].astype(BF16)
            high = saved_hi[rows, :].astype(BF16)
            grad = grad_f[rows, :].astype(BF16)
            saved_h[head, :, :128] = low
            saved_h[head, :, 128:] = high
            grad_h[head] = grad
            product = jnp.concatenate([dot(low, grad, (0, 0)), dot(high, grad, (0, 0))], axis=0).astype(BF16)
            for dp in range(n_dp):
                for ctx in range(2):
                    first = (dp * 2 + ctx) * share
                    vx[ctx, head, dp] = product[first:first + share]
        x_copy(chunk).start()
        return carry

    lax.fori_loop(0, chunks, up_partial, 0)

    lat_copy.wait_recv()
    pos_copy.wait_recv()
    query_pos = pos_in[my_ctx]
    for half in range(2):
        cols = slice(half * slots, (half + 1) * slots)
        block = kt_in[half]
        keys_t[:, cols] = block
        keys[cols, :] = block.astype(F32).T.astype(BF16)
        key_pos = jnp.broadcast_to(pos_in[half], (slots, slots)).T
        bias[cols, :] = jnp.where(key_pos <= query_pos, 0.0, -1e30)
    key_acc[...] = jnp.zeros_like(key_acc)
    up_in.wait()
    q_in.wait()
    lse_in.wait()
    diagonal = lax.broadcasted_iota(jnp.int32, (slots, slots), 0) == lax.broadcasted_iota(
        jnp.int32, (slots, slots), 1)

    def attend(pair):
        one, two = 2 * pair, 2 * pair + 1
        lat_grads, deltas = [], []
        for head in (one, two):
            lat_grad = dot(up_ref[head], grad_h[head], (1, 1)).astype(BF16)
            lat_grads.append(lat_grad)
            full = dot(saved_h[head], lat_grad, (1, 0))
            deltas.append(jnp.sum(jnp.where(diagonal, full, 0.0), axis=0, keepdims=True))
        lat_grad = jnp.concatenate(lat_grads, axis=1)
        delta = jnp.concatenate(deltas, axis=1)
        query = jnp.concatenate([q_ref[one], q_ref[two]], axis=1)
        lse = jnp.concatenate([lse_ref[pl.ds(one, 1), :], lse_ref[pl.ds(two, 1), :]], axis=1)
        mask = jnp.concatenate([bias[...], bias[...]], axis=1)
        logits = dot(keys[...], query, (1, 0)) * scaling
        weights = jnp.exp(logits - lse + mask)
        dot_value = dot(keys[:, :latent], lat_grad, (1, 0))
        dlogits = (weights * (dot_value - delta) * scaling).astype(BF16)
        weights_b = weights.astype(BF16)
        query_grad = dot(keys_t[...], dlogits, (1, 0)).astype(BF16)
        qg_ref[one] = query_grad[:, :slots]
        qg_ref[two] = query_grad[:, slots:]
        key_term = dot(query, dlogits, (1, 1))
        value_term = dot(lat_grad, weights_b, (1, 1))
        key_acc[:latent, :] += key_term[:latent] + value_term
        key_acc[latent:width, :] += key_term[latent:]

    def z_copy(step, chunk, arriving=False):
        peer = lax.rem(my_dp + step, n_dp)
        part = pl.ds(chunk * PER_CHUNK, PER_CHUNK)
        slot = peer if arriving else my_dp
        return send(zs.at[peer, part], zr.at[slot, part], z_send.at[peer, chunk], z_recv.at[slot, chunk], {"dp": peer})

    def forward(chunk):
        x_copy(chunk).wait_recv()
        for offset in range(PER_CHUNK):
            head = chunk * PER_CHUNK + offset
            for dp in range(n_dp):
                zs[dp, head] = (vx[my_ctx, head, dp].astype(F32) + vr[head, dp].astype(F32)).astype(BF16)
        for step in range(1, n_dp):
            z_copy(step, chunk).start()

    def attend_and_forward(pair, carry):
        attend(pair)

        @pl.when(pair >= 1)
        def _():
            forward(pair - 1)

        return carry

    lax.fori_loop(0, chunks, attend_and_forward, 0)
    qg_copy = pltpu.make_async_copy(qg_ref, qg_hbm, out_sem)
    qg_copy.start()

    for part in range(n_head):
        for ctx in range(2):
            ka_send[part, ctx] = key_acc[
                part * piece:(part + 1) * piece, ctx * slots:(ctx + 1) * slots].astype(BF16)
    ka_copies = []
    for step in range(1, n_head):
        to = lax.rem(my_head + step, n_head)
        copy = send(ka_send.at[to], ka_recv.at[my_head], ka_ssem.at[to], ka_rsem.at[my_head], {"head": to})
        copy.start()
        ka_copies.append(copy)

    forward(chunks - 1)

    sums = ka_send[my_head].astype(F32)
    for step in range(1, n_head):
        src = lax.rem(my_head + step, n_head)
        send(ka_send.at[src], ka_recv.at[src], ka_ssem.at[src], ka_rsem.at[src], {"head": src}).wait_recv()
        sums = sums + ka_recv[src].astype(F32)
    kb_send[...] = sums.astype(BF16)
    kb_copy = send(kb_send.at[other], kb_recv, kb_sem.at[0], kb_sem.at[1], {"ctx": other})
    kb_copy.start()

    kb_copy.wait_recv()
    kc[my_head] = (kb_send[my_ctx].astype(F32) + kb_recv[...].astype(F32)).astype(BF16)
    kc_copies = []
    for step in range(1, n_head):
        to = lax.rem(my_head + step, n_head)
        copy = send(kc.at[my_head], kc.at[my_head], kc_ssem.at[to], kc_rsem.at[my_head], {"head": to})
        copy.start()
        kc_copies.append(copy)

    for step in range(1, n_head):
        src = lax.rem(my_head + step, n_head)
        send(kc.at[src], kc.at[src], kc_ssem.at[src], kc_rsem.at[src], {"head": src}).wait_recv()
    for part in range(n_head):
        first, last = part * piece, min((part + 1) * piece, width)
        lg_out[first:last, :] = kc[part, :last - first, :].astype(F32)

    def finish(chunk, carry):
        for step in range(1, n_dp):
            z_copy(step, chunk, arriving=True).wait_recv()
        for offset in range(PER_CHUNK):
            head = chunk * PER_CHUNK + offset
            total = zs[my_dp, head].astype(F32)
            for step in range(1, n_dp):
                total = total + zr[lax.rem(my_dp + step, n_dp), head].astype(F32)
            vg_out[pl.ds(head, share, heads), :] = total
        return carry

    lax.fori_loop(0, chunks, finish, 0)

    def drain(chunk, carry):
        x_copy(chunk).wait_send()
        for step in range(1, n_dp):
            z_copy(step, chunk).wait_send()
        return carry

    lax.fori_loop(0, chunks, drain, 0)
    for copy in [lat_copy, pos_copy, kb_copy] + ka_copies + kc_copies:
        copy.wait_send()
    qg_copy.wait()


def write_out(*refs):
    count = len(refs) // 2
    sems = refs[-1]
    copies = [pltpu.make_async_copy(refs[i], refs[count + i], sems.at[i]) for i in range(count)]
    for copy in copies:
        copy.start()
    for copy in copies:
        copy.wait()


def fused(mesh, queries, latents, positions, lse, saved_out, out_grad, value_up):
    n_dp, n_head = mesh.shape["dp"], mesh.shape["head"]
    _, slots, heads, width = queries.shape
    latent = saved_out.shape[3]
    vhead = out_grad.shape[3]
    share = latent // (n_dp * 2)
    unit = 16 * n_head
    piece = -(-width // unit) * 16
    dims = (n_dp, n_head, heads, slots, width, latent, share)
    dma = pltpu.SemaphoreType.DMA
    chunks = heads // PER_CHUNK
    results = pl.pallas_call(
        functools.partial(kernel, dims),
        out_shape=(
            jax.ShapeDtypeStruct((heads, width, slots), BF16),
            jax.ShapeDtypeStruct((width, slots), F32),
            jax.ShapeDtypeStruct((share * heads, vhead), F32),
        ),
        in_specs=[pl.BlockSpec(memory_space=pltpu.HBM)] * 7,
        out_specs=(
            pl.BlockSpec(memory_space=pl.ANY),
            pl.BlockSpec(memory_space=pltpu.VMEM),
            pl.BlockSpec(memory_space=pltpu.VMEM),
        ),
        scratch_shapes=[
            pltpu.VMEM((heads, width, slots), BF16),
            pltpu.VMEM((2, width, slots), BF16),
            pltpu.VMEM((2, 1, slots), jnp.int32),
            pltpu.VMEM((heads, slots), F32),
            pltpu.VMEM((slots * heads, latent), BF16),
            pltpu.VMEM((slots * heads, vhead), BF16),
            pltpu.VMEM((heads, latent, vhead), BF16),
            pltpu.VMEM((slots * heads, 128), F32),
            pltpu.VMEM((slots * heads, 128), F32),
            pltpu.VMEM((slots * heads, vhead), F32),
            pltpu.VMEM((heads, slots, latent), BF16),
            pltpu.VMEM((heads, slots, vhead), BF16),
            pltpu.VMEM((2 * slots, width), BF16),
            pltpu.VMEM((width, 2 * slots), BF16),
            pltpu.VMEM((2 * slots, slots), F32),
            pltpu.VMEM((2, heads, n_dp, share, vhead), BF16),
            pltpu.VMEM((heads, n_dp, share, vhead), BF16),
            pltpu.VMEM((n_dp, heads, share, vhead), BF16),
            pltpu.VMEM((n_dp, heads, share, vhead), BF16),
            pltpu.VMEM((piece * n_head, 2 * slots), F32),
            pltpu.VMEM((n_head, 2, piece, slots), BF16),
            pltpu.VMEM((n_head, 2, piece, slots), BF16),
            pltpu.VMEM((2, piece, slots), BF16),
            pltpu.VMEM((piece, slots), BF16),
            pltpu.VMEM((n_head, piece, slots), BF16),
            pltpu.VMEM((heads, width, slots), BF16),
            dma((7,)),
            dma((2,)), dma((2,)),
            dma((chunks,)), dma((chunks,)),
            dma((n_dp, chunks)), dma((n_dp, chunks)),
            dma((n_head,)), dma((n_head,)),
            dma((2,)),
            dma((n_head,)), dma((n_head,)),
            dma,
        ],
        compiler_params=pltpu.CompilerParams(
            collective_id=0, has_side_effects=True, vmem_limit_bytes=64 * 1024 * 1024),
    )(
        jnp.transpose(queries[0], (1, 2, 0)),
        latents[0].T,
        positions,
        lse[0].T,
        saved_out.reshape(slots * heads, latent),
        out_grad.reshape(slots * heads, vhead),
        value_up,
    )
    query_grad, latent_grad, up_grad = pl.pallas_call(
        write_out,
        out_shape=tuple(jax.ShapeDtypeStruct(r.shape, r.dtype) for r in results),
        in_specs=[pl.BlockSpec(memory_space=pl.ANY)] * 3,
        out_specs=(pl.BlockSpec(memory_space=pl.ANY),) * 3,
        scratch_shapes=[dma((3,))],
        compiler_params=pltpu.CompilerParams(vmem_limit_bytes=64 * 1024 * 1024),
    )(*results)
    return (
        jnp.transpose(query_grad, (2, 0, 1))[None],
        latent_grad.T[None],
        up_grad.reshape(share, heads, vhead),
    )


def spans(length):
    return [(lower, min(length, lower + 512)) for lower in range(0, length, 512)]


def spread(queries, latents, positions, lse, saved_out, out_grad, value_up):
    query_rows = queries[0]
    slot_count = query_rows.shape[0]
    head_count = query_rows.shape[1]
    full_width = query_rows.shape[2]
    latent_width = saved_out.shape[3]
    query_pos = positions[0]
    row_lse = lse[0]
    latest = jnp.max(query_pos)
    scaling = (VHEAD + ROPE) ** (-0.5)
    lat_grad = jnp.einsum(
        "thv,hlv->thl", out_grad[0], value_up, preferred_element_type=jnp.float32
    ).astype(jnp.bfloat16)
    row_delta = jnp.sum(lat_grad.astype(jnp.float32) * saved_out[0].astype(jnp.float32), axis=-1)
    slab_rows = slot_count * lax.axis_size("ctx")
    carry = (
        jnp.zeros((slot_count, head_count, full_width), jnp.float32),
        jnp.zeros((slab_rows, full_width), jnp.float32),
    )
    keys_in = lax.all_gather(latents[0], "ctx", axis=0, tiled=True)
    pos_in = lax.all_gather(positions[0], "ctx", axis=0, tiled=True)
    for lower, upper in spans(keys_in.shape[0]):
        key_rows = keys_in[lower:upper]
        key_pos = pos_in[lower:upper]

        def update(state):
            query_acc, key_acc = state
            logits = (
                jnp.einsum("thd,kd->thk", query_rows, key_rows, preferred_element_type=jnp.float32)
                * scaling
            )
            visible = key_pos[None, None, :] <= query_pos[:, None, None]
            weights = jnp.where(visible, jnp.exp(logits - row_lse[:, :, None]), 0.0)
            dot_value = jnp.einsum(
                "thl,kl->thk",
                lat_grad,
                key_rows[:, :latent_width],
                preferred_element_type=jnp.float32,
            )
            dlogits = (weights * (dot_value - row_delta[:, :, None]) * scaling).astype(jnp.bfloat16)
            query_acc = query_acc + jnp.einsum(
                "thk,kd->thd", dlogits, key_rows, preferred_element_type=jnp.float32
            )
            key_term = jnp.einsum(
                "thk,thd->kd", dlogits, query_rows, preferred_element_type=jnp.float32
            )
            value_term = jnp.einsum(
                "thk,thl->kl",
                weights.astype(jnp.bfloat16),
                lat_grad,
                preferred_element_type=jnp.float32,
            )
            key_term = key_term + jnp.pad(value_term, ((0, 0), (0, full_width - latent_width)))
            previous = lax.dynamic_slice_in_dim(key_acc, 0 + lower, upper - lower, 0)
            key_acc = lax.dynamic_update_slice_in_dim(key_acc, previous + key_term, 0 + lower, 0)
            return (query_acc, key_acc)

        carry = lax.cond(jnp.min(key_pos) > latest, lambda state: state, update, carry)
    query_acc, key_acc = carry
    summed = lax.psum(key_acc, "head")
    own_rows = lax.psum_scatter(summed, "ctx", scatter_dimension=0, tiled=True)
    weight_share = lax.psum_scatter(
        jnp.einsum("thl,thv->lhv", saved_out[0], out_grad[0], preferred_element_type=jnp.float32),
        ("dp", "ctx"),
        scatter_dimension=0,
        tiled=True,
    )
    return (query_acc.astype(jnp.bfloat16)[None], own_rows[None], weight_share)


def solution(mesh):
    body = functools.partial(fused, mesh) if mesh.shape["ctx"] == 2 else spread
    return jax.shard_map(
        body,
        mesh=mesh,
        in_specs=(
            P("dp", "ctx", "head", None),
            P("dp", "ctx", None),
            P("dp", "ctx"),
            P("dp", "ctx", "head"),
            P("dp", "ctx", "head", None),
            P("dp", "ctx", "head", None),
            P("head", None, None),
        ),
        out_specs=(
            P("dp", "ctx", "head", None),
            P("dp", "ctx", None),
            P(("dp", "ctx"), "head", None),
        ),
        check_vma=False,
    )
```

```python
import functools

import jax
import jax.numpy as jnp
from jax import lax
from jax.experimental import pallas as pl
from jax.experimental.pallas import tpu as pltpu
from jax.sharding import PartitionSpec as P

ROPE = 32
VHEAD = 128
MESH = pl.DeviceIdType.MESH
BF16 = jnp.bfloat16
F32 = jnp.float32
PER_CHUNK = 4


def dot(lhs, rhs, over):
    return lax.dot_general(lhs, rhs, (((over[0],), (over[1],)), ((), ())), preferred_element_type=F32)


def slab_peers(my_ctx, my_head, n_head):
    ahead = [{"ctx": my_ctx, "head": lax.rem(my_head + step, n_head)} for step in range(1, n_head)]
    across = [{"ctx": 1 - my_ctx, "head": lax.rem(my_head + step, n_head)} for step in range(n_head)]
    return across + ahead


def kernel(
    dims,
    q_hbm, lat_hbm, pos_hbm, lse_hbm, saved_hbm, grad_hbm, up_hbm,
    qg_hbm, lg_out, vg_out,
    q_ref, kt_in, pos_in, lse_ref, saved_b, grad_b, up_ref,
    saved_lo, saved_hi, grad_f, lat_grads, deltas, dlogits_all,
    keys, keys_t, bias,
    vx, vr, zs, zr,
    key_acc, ka_send, ka_recv, kc,
    qg_ref,
    in_sem, lat_send, lat_recv, x_send, x_recv, z_send, z_recv,
    ka_ssem, ka_rsem, kc_ssem, kc_rsem, out_sem,
):
    n_dp, n_head, heads, slots, width, latent, share = dims
    scaling = (VHEAD + ROPE) ** -0.5
    my_dp, my_ctx, my_head = lax.axis_index("dp"), lax.axis_index("ctx"), lax.axis_index("head")
    other = 1 - my_ctx
    chunks = heads // PER_CHUNK
    piece = key_acc.shape[0] // n_head

    def load(index, source, target):
        copy = pltpu.make_async_copy(source, target, in_sem.at[index])
        copy.start()
        return copy

    lat_in = load(0, lat_hbm, kt_in.at[my_ctx])
    pos_load = load(1, pos_hbm, pos_in.at[my_ctx])
    saved_in = load(2, saved_hbm, saved_b)
    grad_in = load(3, grad_hbm, grad_b)
    up_in = load(4, up_hbm, up_ref)
    q_in = load(5, q_hbm, q_ref)
    lse_in = load(6, lse_hbm, lse_ref)

    barrier = pltpu.get_barrier_semaphore()
    for step in range(1, n_dp):
        pl.semaphore_signal(barrier, inc=1, device_id={"dp": lax.rem(my_dp + step, n_dp)}, device_id_type=MESH)
    for where in slab_peers(my_ctx, my_head, n_head):
        pl.semaphore_signal(barrier, inc=1, device_id=where, device_id_type=MESH)
    lat_in.wait()
    pos_load.wait()
    pl.semaphore_wait(barrier, (n_dp - 1) + (2 * n_head - 1))

    def send(source, target, send_sem, recv_sem, where):
        return pltpu.make_async_remote_copy(
            src_ref=source, dst_ref=target, send_sem=send_sem, recv_sem=recv_sem,
            device_id=where, device_id_type=MESH)

    lat_copy = send(kt_in.at[my_ctx], kt_in.at[my_ctx], lat_send.at[0], lat_recv.at[0], {"ctx": other})
    pos_copy = send(pos_in.at[my_ctx], pos_in.at[my_ctx], lat_send.at[1], lat_recv.at[1], {"ctx": other})
    lat_copy.start()
    pos_copy.start()

    saved_in.wait()
    grad_in.wait()
    rows_step = (slots * heads) // 8

    def widen(step, carry):
        rows = pl.ds(pl.multiple_of(step * rows_step, rows_step), rows_step)
        saved_lo[rows, :] = saved_b[rows, :128].astype(F32)
        saved_hi[rows, :] = saved_b[rows, 128:].astype(F32)
        grad_f[rows, :] = grad_b[rows, :].astype(F32)
        return carry

    lax.fori_loop(0, 8, widen, 0)

    def x_copy(chunk):
        part = pl.ds(chunk * PER_CHUNK, PER_CHUNK)
        return send(vx.at[other, part], vr.at[part], x_send.at[chunk], x_recv.at[chunk], {"ctx": other})

    diagonal = lax.broadcasted_iota(jnp.int32, (slots, slots), 0) == lax.broadcasted_iota(
        jnp.int32, (slots, slots), 1)
    up_in.wait()

    def up_partial(chunk, carry):
        members = [chunk * PER_CHUNK + offset for offset in range(PER_CHUNK)]
        lows, highs, grads = [], [], []
        for head in members:
            rows = pl.ds(head, slots, heads)
            lows.append(saved_lo[rows, :].astype(BF16))
            highs.append(saved_hi[rows, :].astype(BF16))
            grads.append(grad_f[rows, :].astype(BF16))
        for head, low, high, grad in zip(members, lows, highs, grads):
            product = jnp.concatenate([dot(low, grad, (0, 0)), dot(high, grad, (0, 0))], axis=0).astype(BF16)
            for dp in range(n_dp):
                for ctx in range(2):
                    first = (dp * 2 + ctx) * share
                    vx[ctx, head, dp] = product[first:first + share]
        x_copy(chunk).start()
        raised = [dot(up_ref[head], grad, (1, 1)).astype(BF16) for head, grad in zip(members, grads)]
        lat_grads[chunk] = jnp.concatenate(raised, axis=1)
        sums = []
        for low, high, lat_grad in zip(lows, highs, raised):
            full = dot(jnp.concatenate([low, high], axis=1), lat_grad, (1, 0))
            sums.append(jnp.sum(jnp.where(diagonal, full, 0.0), axis=0, keepdims=True))
        deltas[chunk] = jnp.concatenate(sums, axis=1)
        return carry

    lax.fori_loop(0, chunks, up_partial, 0)

    lat_copy.wait_recv()
    pos_copy.wait_recv()
    query_pos = pos_in[my_ctx]
    for half in range(2):
        cols = slice(half * slots, (half + 1) * slots)
        block = kt_in[half]
        keys_t[:, cols] = block
        keys[cols, :] = block.astype(F32).T.astype(BF16)
        key_pos = jnp.broadcast_to(pos_in[half], (slots, slots)).T
        bias[cols, :] = jnp.where(key_pos <= query_pos, 0.0, -1e30)
    key_acc[...] = jnp.zeros_like(key_acc)
    q_in.wait()
    lse_in.wait()

    def attend(chunk):
        members = [chunk * PER_CHUNK + offset for offset in range(PER_CHUNK)]
        query = jnp.concatenate([q_ref[head] for head in members], axis=1)
        lse = jnp.concatenate([lse_ref[pl.ds(head, 1), :] for head in members], axis=1)
        mask = jnp.concatenate([bias[...]] * PER_CHUNK, axis=1)
        lat_grad = lat_grads[chunk]
        logits = dot(keys[...], query, (1, 0)) * scaling
        dot_value = dot(keys[:, :latent], lat_grad, (1, 0))
        weights = jnp.exp(logits - lse + mask)
        dlogits = (weights * (dot_value - deltas[chunk]) * scaling).astype(BF16)
        dlogits_all[chunk] = dlogits
        key_term = dot(query, dlogits, (1, 1))
        value_term = dot(lat_grad, weights.astype(BF16), (1, 1))
        key_acc[:latent, :] += key_term[:latent] + value_term
        key_acc[latent:width, :] += key_term[latent:]

    def z_copy(step, chunk, arriving=False):
        peer = lax.rem(my_dp + step, n_dp)
        part = pl.ds(chunk * PER_CHUNK, PER_CHUNK)
        slot = peer if arriving else my_dp
        return send(zs.at[peer, part], zr.at[slot, part], z_send.at[peer, chunk], z_recv.at[slot, chunk], {"dp": peer})

    def forward(chunk):
        x_copy(chunk).wait_recv()
        for offset in range(PER_CHUNK):
            head = chunk * PER_CHUNK + offset
            for dp in range(n_dp):
                zs[dp, head] = (vx[my_ctx, head, dp].astype(F32) + vr[head, dp].astype(F32)).astype(BF16)
        for step in range(1, n_dp):
            z_copy(step, chunk).start()

    def attend_and_forward(chunk, carry):
        attend(chunk)

        @pl.when(chunk < chunks - 1)
        def _():
            forward(chunk)

        return carry

    lax.fori_loop(0, chunks, attend_and_forward, 0)

    for ctx in range(2):
        for part in range(n_head):
            ka_send[ctx, part] = key_acc[
                part * piece:(part + 1) * piece, ctx * slots:(ctx + 1) * slots].astype(BF16)

    def ka_copy(where, arriving=False):
        theirs, mine = (where["ctx"], where["head"]), (my_ctx, my_head)
        slot = theirs if arriving else mine
        return send(ka_send.at[theirs], ka_recv.at[slot], ka_ssem.at[theirs], ka_rsem.at[slot], where)

    peers = slab_peers(my_ctx, my_head, n_head)
    for where in peers:
        ka_copy(where).start()

    forward(chunks - 1)

    def query_grads(chunk, carry):
        query_grad = dot(keys_t[...], dlogits_all[chunk], (1, 0)).astype(BF16)
        for offset in range(PER_CHUNK):
            qg_ref[chunk * PER_CHUNK + offset] = query_grad[:, offset * slots:(offset + 1) * slots]
        return carry

    lax.fori_loop(0, chunks, query_grads, 0)
    qg_copy = pltpu.make_async_copy(qg_ref, qg_hbm, out_sem)
    qg_copy.start()

    sums = ka_send[my_ctx, my_head].astype(F32)
    for where in peers:
        ka_copy(where, arriving=True).wait_recv()
        sums = sums + ka_recv[where["ctx"], where["head"]].astype(F32)
    kc[my_head] = sums.astype(BF16)
    kc_copies = []
    for step in range(1, n_head):
        to = lax.rem(my_head + step, n_head)
        copy = send(kc.at[my_head], kc.at[my_head], kc_ssem.at[to], kc_rsem.at[my_head], {"head": to})
        copy.start()
        kc_copies.append(copy)

    def finish(chunk, carry):
        for step in range(1, n_dp):
            z_copy(step, chunk, arriving=True).wait_recv()
        for offset in range(PER_CHUNK):
            head = chunk * PER_CHUNK + offset
            total = zs[my_dp, head].astype(F32)
            for step in range(1, n_dp):
                total = total + zr[lax.rem(my_dp + step, n_dp), head].astype(F32)
            vg_out[pl.ds(head, share, heads), :] = total
        return carry

    lax.fori_loop(0, chunks, finish, 0)

    for step in range(1, n_head):
        src = lax.rem(my_head + step, n_head)
        send(kc.at[src], kc.at[src], kc_ssem.at[src], kc_rsem.at[src], {"head": src}).wait_recv()
    for part in range(n_head):
        first, last = part * piece, min((part + 1) * piece, width)
        lg_out[first:last, :] = kc[part, :last - first, :].astype(F32)

    def drain(chunk, carry):
        x_copy(chunk).wait_send()
        for step in range(1, n_dp):
            z_copy(step, chunk).wait_send()
        return carry

    lax.fori_loop(0, chunks, drain, 0)
    for copy in [lat_copy, pos_copy] + [ka_copy(where) for where in peers] + kc_copies:
        copy.wait_send()
    qg_copy.wait()


def write_out(*refs):
    sources, targets, rooms, (in_sem, out_sem) = refs[:3], refs[3:6], refs[6:9], refs[9:]
    pieces = []
    for source, target, room in zip(sources, targets, rooms):
        count = 4 if source.ndim == 3 else 1
        size = source.shape[0] // count
        for part in range(count):
            rows = pl.ds(part * size, size)
            index = len(pieces)
            pieces.append((
                pltpu.make_async_copy(source.at[rows], room.at[rows], in_sem.at[index]),
                pltpu.make_async_copy(room.at[rows], target.at[rows], out_sem.at[index])))
    for come, _ in pieces:
        come.start()
    for come, leave in pieces:
        come.wait()
        leave.start()
    for _, leave in pieces:
        leave.wait()


def fused(mesh, queries, latents, positions, lse, saved_out, out_grad, value_up):
    n_dp, n_head = mesh.shape["dp"], mesh.shape["head"]
    _, slots, heads, width = queries.shape
    latent = saved_out.shape[3]
    vhead = out_grad.shape[3]
    share = latent // (n_dp * 2)
    unit = 16 * n_head
    piece = -(-width // unit) * 16
    dims = (n_dp, n_head, heads, slots, width, latent, share)
    dma = pltpu.SemaphoreType.DMA
    chunks = heads // PER_CHUNK
    results = pl.pallas_call(
        functools.partial(kernel, dims),
        out_shape=(
            jax.ShapeDtypeStruct((heads, width, slots), BF16),
            jax.ShapeDtypeStruct((width, slots), F32),
            jax.ShapeDtypeStruct((share * heads, vhead), F32),
        ),
        in_specs=[pl.BlockSpec(memory_space=pltpu.HBM)] * 7,
        out_specs=(
            pl.BlockSpec(memory_space=pl.ANY),
            pl.BlockSpec(memory_space=pltpu.VMEM),
            pl.BlockSpec(memory_space=pltpu.VMEM),
        ),
        scratch_shapes=[
            pltpu.VMEM((heads, width, slots), BF16),
            pltpu.VMEM((2, width, slots), BF16),
            pltpu.VMEM((2, 1, slots), jnp.int32),
            pltpu.VMEM((heads, slots), F32),
            pltpu.VMEM((slots * heads, latent), BF16),
            pltpu.VMEM((slots * heads, vhead), BF16),
            pltpu.VMEM((heads, latent, vhead), BF16),
            pltpu.VMEM((slots * heads, 128), F32),
            pltpu.VMEM((slots * heads, 128), F32),
            pltpu.VMEM((slots * heads, vhead), F32),
            pltpu.VMEM((chunks, latent, PER_CHUNK * slots), BF16),
            pltpu.VMEM((chunks, 1, PER_CHUNK * slots), F32),
            pltpu.VMEM((chunks, 2 * slots, PER_CHUNK * slots), BF16),
            pltpu.VMEM((2 * slots, width), BF16),
            pltpu.VMEM((width, 2 * slots), BF16),
            pltpu.VMEM((2 * slots, slots), F32),
            pltpu.VMEM((2, heads, n_dp, share, vhead), BF16),
            pltpu.VMEM((heads, n_dp, share, vhead), BF16),
            pltpu.VMEM((n_dp, heads, share, vhead), BF16),
            pltpu.VMEM((n_dp, heads, share, vhead), BF16),
            pltpu.VMEM((piece * n_head, 2 * slots), F32),
            pltpu.VMEM((2, n_head, piece, slots), BF16),
            pltpu.VMEM((2, n_head, piece, slots), BF16),
            pltpu.VMEM((n_head, piece, slots), BF16),
            pltpu.VMEM((heads, width, slots), BF16),
            dma((7,)),
            dma((2,)), dma((2,)),
            dma((chunks,)), dma((chunks,)),
            dma((n_dp, chunks)), dma((n_dp, chunks)),
            dma((2, n_head)), dma((2, n_head)),
            dma((n_head,)), dma((n_head,)),
            dma,
        ],
        compiler_params=pltpu.CompilerParams(
            collective_id=0, has_side_effects=True, vmem_limit_bytes=64 * 1024 * 1024),
    )(
        jnp.transpose(queries[0], (1, 2, 0)),
        latents[0].T,
        positions,
        lse[0].T,
        saved_out.reshape(slots * heads, latent),
        out_grad.reshape(slots * heads, vhead),
        value_up,
    )
    query_grad, latent_grad, up_grad = pl.pallas_call(
        write_out,
        out_shape=tuple(jax.ShapeDtypeStruct(r.shape, r.dtype) for r in results),
        in_specs=[pl.BlockSpec(memory_space=pl.ANY)] * 3,
        out_specs=(pl.BlockSpec(memory_space=pl.ANY),) * 3,
        scratch_shapes=[pltpu.VMEM(r.shape, r.dtype) for r in results] + [dma((6,)), dma((6,))],
        compiler_params=pltpu.CompilerParams(vmem_limit_bytes=64 * 1024 * 1024),
    )(*results)
    return (
        jnp.transpose(query_grad, (2, 0, 1))[None],
        latent_grad.T[None],
        up_grad.reshape(share, heads, vhead),
    )


def spans(length):
    return [(lower, min(length, lower + 512)) for lower in range(0, length, 512)]


def spread(queries, latents, positions, lse, saved_out, out_grad, value_up):
    query_rows = queries[0]
    slot_count = query_rows.shape[0]
    head_count = query_rows.shape[1]
    full_width = query_rows.shape[2]
    latent_width = saved_out.shape[3]
    query_pos = positions[0]
    row_lse = lse[0]
    latest = jnp.max(query_pos)
    scaling = (VHEAD + ROPE) ** (-0.5)
    lat_grad = jnp.einsum(
        "thv,hlv->thl", out_grad[0], value_up, preferred_element_type=jnp.float32
    ).astype(jnp.bfloat16)
    row_delta = jnp.sum(lat_grad.astype(jnp.float32) * saved_out[0].astype(jnp.float32), axis=-1)
    slab_rows = slot_count * lax.axis_size("ctx")
    carry = (
        jnp.zeros((slot_count, head_count, full_width), jnp.float32),
        jnp.zeros((slab_rows, full_width), jnp.float32),
    )
    keys_in = lax.all_gather(latents[0], "ctx", axis=0, tiled=True)
    pos_in = lax.all_gather(positions[0], "ctx", axis=0, tiled=True)
    for lower, upper in spans(keys_in.shape[0]):
        key_rows = keys_in[lower:upper]
        key_pos = pos_in[lower:upper]

        def update(state):
            query_acc, key_acc = state
            logits = (
                jnp.einsum("thd,kd->thk", query_rows, key_rows, preferred_element_type=jnp.float32)
                * scaling
            )
            visible = key_pos[None, None, :] <= query_pos[:, None, None]
            weights = jnp.where(visible, jnp.exp(logits - row_lse[:, :, None]), 0.0)
            dot_value = jnp.einsum(
                "thl,kl->thk",
                lat_grad,
                key_rows[:, :latent_width],
                preferred_element_type=jnp.float32,
            )
            dlogits = (weights * (dot_value - row_delta[:, :, None]) * scaling).astype(jnp.bfloat16)
            query_acc = query_acc + jnp.einsum(
                "thk,kd->thd", dlogits, key_rows, preferred_element_type=jnp.float32
            )
            key_term = jnp.einsum(
                "thk,thd->kd", dlogits, query_rows, preferred_element_type=jnp.float32
            )
            value_term = jnp.einsum(
                "thk,thl->kl",
                weights.astype(jnp.bfloat16),
                lat_grad,
                preferred_element_type=jnp.float32,
            )
            key_term = key_term + jnp.pad(value_term, ((0, 0), (0, full_width - latent_width)))
            previous = lax.dynamic_slice_in_dim(key_acc, 0 + lower, upper - lower, 0)
            key_acc = lax.dynamic_update_slice_in_dim(key_acc, previous + key_term, 0 + lower, 0)
            return (query_acc, key_acc)

        carry = lax.cond(jnp.min(key_pos) > latest, lambda state: state, update, carry)
    query_acc, key_acc = carry
    summed = lax.psum(key_acc, "head")
    own_rows = lax.psum_scatter(summed, "ctx", scatter_dimension=0, tiled=True)
    weight_share = lax.psum_scatter(
        jnp.einsum("thl,thv->lhv", saved_out[0], out_grad[0], preferred_element_type=jnp.float32),
        ("dp", "ctx"),
        scatter_dimension=0,
        tiled=True,
    )
    return (query_acc.astype(jnp.bfloat16)[None], own_rows[None], weight_share)


def solution(mesh):
    body = functools.partial(fused, mesh) if mesh.shape["ctx"] == 2 else spread
    return jax.shard_map(
        body,
        mesh=mesh,
        in_specs=(
            P("dp", "ctx", "head", None),
            P("dp", "ctx", None),
            P("dp", "ctx"),
            P("dp", "ctx", "head"),
            P("dp", "ctx", "head", None),
            P("dp", "ctx", "head", None),
            P("head", None, None),
        ),
        out_specs=(
            P("dp", "ctx", "head", None),
            P("dp", "ctx", None),
            P(("dp", "ctx"), "head", None),
        ),
        check_vma=False,
    )
```

```python
import functools

import jax
import jax.numpy as jnp
from jax import lax
from jax.experimental import pallas as pl
from jax.experimental.pallas import tpu as pltpu
from jax.sharding import PartitionSpec as P

ROPE = 32
VHEAD = 128
MESH = pl.DeviceIdType.MESH
BF16 = jnp.bfloat16
F32 = jnp.float32
PER_CHUNK = 2
PER_STEP = 4


def dot(lhs, rhs, over):
    return lax.dot_general(lhs, rhs, (((over[0],), (over[1],)), ((), ())), preferred_element_type=F32)


def kernel(
    dims,
    q_hbm, lat_hbm, pos_hbm, lse_hbm, saved_hbm, grad_hbm, up_hbm,
    qg_hbm, lg_hbm, vg_hbm,
    q_ref, kt_in, pos_in, lse_ref, saved_b, grad_b, up_ref,
    saved_lo, saved_hi, grad_f, saved_h, grad_h, lat_grads, deltas, dlogits_all,
    keys, keys_t, bias,
    vx, vr, zs, zr,
    key_acc, ka_send, ka_recv, kb_send, kb_recv, kc,
    qg_ref, lg_ref, vg_ref,
    in_sem, lat_send, lat_recv, x_send, x_recv, z_send, z_recv,
    ka_ssem, ka_rsem, kb_sem, kc_ssem, kc_rsem, out_sem, vg_sem,
):
    n_dp, n_head, heads, slots, width, latent, share = dims
    scaling = (VHEAD + ROPE) ** -0.5
    my_dp, my_ctx, my_head = lax.axis_index("dp"), lax.axis_index("ctx"), lax.axis_index("head")
    other = 1 - my_ctx
    chunks, steps, ratio = heads // PER_CHUNK, heads // PER_STEP, PER_STEP // PER_CHUNK
    piece = key_acc.shape[0] // n_head

    def load(index, source, target):
        copy = pltpu.make_async_copy(source, target, in_sem.at[index])
        copy.start()
        return copy

    lat_in = load(0, lat_hbm, kt_in.at[my_ctx])
    pos_load = load(1, pos_hbm, pos_in.at[my_ctx])
    saved_in = load(2, saved_hbm, saved_b)
    grad_in = load(3, grad_hbm, grad_b)

    barrier = pltpu.get_barrier_semaphore()
    for step in range(1, n_dp):
        pl.semaphore_signal(barrier, inc=1, device_id={"dp": lax.rem(my_dp + step, n_dp)}, device_id_type=MESH)
    for step in range(1, n_head):
        pl.semaphore_signal(barrier, inc=1, device_id={"head": lax.rem(my_head + step, n_head)}, device_id_type=MESH)
    pl.semaphore_signal(barrier, inc=1, device_id={"ctx": other}, device_id_type=MESH)

    def send(source, target, send_sem, recv_sem, where):
        return pltpu.make_async_remote_copy(
            src_ref=source, dst_ref=target, send_sem=send_sem, recv_sem=recv_sem,
            device_id=where, device_id_type=MESH)

    saved_in.wait()
    grad_in.wait()
    up_in = load(4, up_hbm, up_ref)
    q_in = load(5, q_hbm, q_ref)
    lse_in = load(6, lse_hbm, lse_ref)
    rows_step = (slots * heads) // 8

    def widen(step, carry):
        rows = pl.ds(pl.multiple_of(step * rows_step, rows_step), rows_step)
        saved_lo[rows, :] = saved_b[rows, :128].astype(F32)
        saved_hi[rows, :] = saved_b[rows, 128:].astype(F32)
        grad_f[rows, :] = grad_b[rows, :].astype(F32)
        return carry

    lax.fori_loop(0, 8, widen, 0)

    lat_in.wait()
    pos_load.wait()
    pl.semaphore_wait(barrier, (n_dp - 1) + (n_head - 1) + 1)
    lat_copy = send(kt_in.at[my_ctx], kt_in.at[my_ctx], lat_send.at[0], lat_recv.at[0], {"ctx": other})
    pos_copy = send(pos_in.at[my_ctx], pos_in.at[my_ctx], lat_send.at[1], lat_recv.at[1], {"ctx": other})
    lat_copy.start()
    pos_copy.start()

    def x_copy(chunk):
        part = pl.ds(chunk * PER_CHUNK, PER_CHUNK)
        return send(vx.at[other, part], vr.at[part], x_send.at[chunk], x_recv.at[chunk], {"ctx": other})

    def up_partial(step, carry):
        for part in range(ratio):
            chunk = step * ratio + part
            for offset in range(PER_CHUNK):
                head = chunk * PER_CHUNK + offset
                rows = pl.ds(head, slots, heads)
                low = saved_lo[rows, :].astype(BF16)
                high = saved_hi[rows, :].astype(BF16)
                grad = grad_f[rows, :].astype(BF16)
                saved_h[head, :, :128] = low
                saved_h[head, :, 128:] = high
                grad_h[head] = grad
                product = jnp.concatenate([dot(low, grad, (0, 0)), dot(high, grad, (0, 0))], axis=0).astype(BF16)
                for dp in range(n_dp):
                    for ctx in range(2):
                        first = (dp * 2 + ctx) * share
                        vx[ctx, head, dp] = product[first:first + share]
            x_copy(chunk).start()
        return carry

    lax.fori_loop(0, steps, up_partial, 0)

    diagonal = lax.broadcasted_iota(jnp.int32, (slots, slots), 0) == lax.broadcasted_iota(
        jnp.int32, (slots, slots), 1)
    up_in.wait()

    def raise_grads(step, carry):
        members = [step * PER_STEP + offset for offset in range(PER_STEP)]
        raised = [dot(up_ref[head], grad_h[head], (1, 1)).astype(BF16) for head in members]
        lat_grads[step] = jnp.concatenate(raised, axis=1)
        sums = []
        for head, lat_grad in zip(members, raised):
            full = dot(saved_h[head], lat_grad, (1, 0))
            sums.append(jnp.sum(jnp.where(diagonal, full, 0.0), axis=0, keepdims=True))
        deltas[step] = jnp.concatenate(sums, axis=1)
        return carry

    lax.fori_loop(0, steps, raise_grads, 0)

    lat_copy.wait_recv()
    pos_copy.wait_recv()
    query_pos = pos_in[my_ctx]
    for half in range(2):
        cols = slice(half * slots, (half + 1) * slots)
        block = kt_in[half]
        keys_t[:, cols] = block
        keys[cols, :] = block.astype(F32).T.astype(BF16)
        key_pos = jnp.broadcast_to(pos_in[half], (slots, slots)).T
        bias[cols, :] = jnp.where(key_pos <= query_pos, 0.0, -1e30)
    key_acc[...] = jnp.zeros_like(key_acc)
    q_in.wait()
    lse_in.wait()

    def attend(step):
        members = [step * PER_STEP + offset for offset in range(PER_STEP)]
        query = jnp.concatenate([q_ref[head] for head in members], axis=1)
        lse = jnp.concatenate([lse_ref[pl.ds(head, 1), :] for head in members], axis=1)
        mask = jnp.concatenate([bias[...]] * PER_STEP, axis=1)
        lat_grad = lat_grads[step]
        logits = dot(keys[...], query, (1, 0)) * scaling
        dot_value = dot(keys[:, :latent], lat_grad, (1, 0))
        weights = jnp.exp(logits - lse + mask)
        dlogits = (weights * (dot_value - deltas[step]) * scaling).astype(BF16)
        dlogits_all[step] = dlogits
        key_term = dot(query, dlogits, (1, 1))
        value_term = dot(lat_grad, weights.astype(BF16), (1, 1))
        key_acc[:latent, :] += key_term[:latent] + value_term
        key_acc[latent:width, :] += key_term[latent:]

    def z_copy(step, chunk, arriving=False):
        peer = lax.rem(my_dp + step, n_dp)
        part = pl.ds(chunk * PER_CHUNK, PER_CHUNK)
        slot = peer if arriving else my_dp
        return send(zs.at[peer, part], zr.at[slot, part], z_send.at[peer, chunk], z_recv.at[slot, chunk], {"dp": peer})

    def forward(chunk):
        x_copy(chunk).wait_recv()
        for offset in range(PER_CHUNK):
            head = chunk * PER_CHUNK + offset
            for dp in range(n_dp):
                zs[dp, head] = (vx[my_ctx, head, dp].astype(F32) + vr[head, dp].astype(F32)).astype(BF16)
        for step in range(1, n_dp):
            z_copy(step, chunk).start()

    def attend_and_forward(step, carry):
        attend(step)
        for part in range(ratio):
            chunk = step * ratio + part - 1

            @pl.when(chunk >= 0)
            def _():
                forward(chunk)

        return carry

    lax.fori_loop(0, steps - 1, attend_and_forward, 0)
    attend(steps - 1)

    for part in range(n_head):
        for ctx in range(2):
            ka_send[part, ctx] = key_acc[
                part * piece:(part + 1) * piece, ctx * slots:(ctx + 1) * slots].astype(BF16)

    def ka_copy(step, arriving=False):
        peer = lax.rem(my_head + step, n_head)
        slot = peer if arriving else my_head
        return send(ka_send.at[peer], ka_recv.at[slot], ka_ssem.at[peer], ka_rsem.at[slot], {"head": peer})

    def kc_copy(step, arriving=False):
        peer = lax.rem(my_head + step, n_head)
        slot = peer if arriving else my_head
        return send(kc.at[slot], kc.at[slot], kc_ssem.at[peer], kc_rsem.at[slot], {"head": peer})

    for step in range(1, n_head):
        ka_copy(step).start()

    for part in range(ratio):
        forward((steps - 1) * ratio + part - 1)

    def query_grads(step, carry):
        query_grad = dot(keys_t[...], dlogits_all[step], (1, 0)).astype(BF16)
        for offset in range(PER_STEP):
            qg_ref[step * PER_STEP + offset] = query_grad[:, offset * slots:(offset + 1) * slots]
        return carry

    lax.fori_loop(0, steps // 2, query_grads, 0)

    sums = ka_send[my_head].astype(F32)
    for step in range(1, n_head):
        ka_copy(step, arriving=True).wait_recv()
        sums = sums + ka_recv[lax.rem(my_head + step, n_head)].astype(F32)
    kb_send[...] = sums.astype(BF16)
    kb_copy = send(kb_send.at[other], kb_recv, kb_sem.at[0], kb_sem.at[1], {"ctx": other})
    kb_copy.start()

    lax.fori_loop(steps // 2, steps, query_grads, 0)
    qg_copy = pltpu.make_async_copy(qg_ref, qg_hbm, out_sem.at[0])
    qg_copy.start()
    forward(chunks - 1)

    kb_copy.wait_recv()
    kc[my_head] = (kb_send[my_ctx].astype(F32) + kb_recv[...].astype(F32)).astype(BF16)
    for step in range(1, n_head):
        kc_copy(step).start()

    def vg_copy(chunk):
        part = pl.ds(chunk * PER_CHUNK, PER_CHUNK)
        return pltpu.make_async_copy(vg_ref.at[part], vg_hbm.at[part], vg_sem.at[chunk])

    def finish(chunk, carry):
        for step in range(1, n_dp):
            z_copy(step, chunk, arriving=True).wait_recv()
        for offset in range(PER_CHUNK):
            head = chunk * PER_CHUNK + offset
            total = zs[my_dp, head].astype(F32)
            for step in range(1, n_dp):
                total = total + zr[lax.rem(my_dp + step, n_dp), head].astype(F32)
            vg_ref[head] = total
        vg_copy(chunk).start()
        return carry

    lax.fori_loop(0, chunks - ratio, finish, 0)
    for step in range(1, n_head):
        kc_copy(step, arriving=True).wait_recv()
    for part in range(n_head):
        first, last = part * piece, min((part + 1) * piece, width)
        lg_ref[first:last, :] = kc[part, :last - first, :].astype(F32)
    lg_copy = pltpu.make_async_copy(lg_ref, lg_hbm, out_sem.at[1])
    lg_copy.start()
    lax.fori_loop(chunks - ratio, chunks, finish, 0)

    def drain(chunk, carry):
        x_copy(chunk).wait_send()
        for step in range(1, n_dp):
            z_copy(step, chunk).wait_send()
        vg_copy(chunk).wait()
        return carry

    lax.fori_loop(0, chunks, drain, 0)
    for copy in [lat_copy, pos_copy, kb_copy]:
        copy.wait_send()
    for step in range(1, n_head):
        ka_copy(step).wait_send()
        kc_copy(step).wait_send()
    qg_copy.wait()
    lg_copy.wait()


def write_out(qg_hbm, lg_hbm, vg_hbm, qg_out, lg_out, vg_out, qg_ref, lg_ref, vg_ref, vg_rows, in_sem, out_sem):
    heads, share, _ = vg_ref.shape
    come = pltpu.make_async_copy(vg_hbm, vg_ref, in_sem.at[0])
    leave = pltpu.make_async_copy(vg_rows, vg_out, out_sem.at[0])
    pieces = [(
        pltpu.make_async_copy(lg_hbm, lg_ref, in_sem.at[1]),
        pltpu.make_async_copy(lg_ref, lg_out, out_sem.at[1]))]
    size = heads // 4
    for part in range(4):
        rows = pl.ds(part * size, size)
        pieces.append((
            pltpu.make_async_copy(qg_hbm.at[rows], qg_ref.at[rows], in_sem.at[2 + part]),
            pltpu.make_async_copy(qg_ref.at[rows], qg_out.at[rows], out_sem.at[2 + part])))
    come.start()
    for first, _ in pieces:
        first.start()
    come.wait()
    for head in range(heads):
        vg_rows[pl.ds(head, share, heads), :] = vg_ref[head]
    leave.start()
    for first, second in pieces:
        first.wait()
        second.start()
    leave.wait()
    for _, second in pieces:
        second.wait()


def fused(mesh, queries, latents, positions, lse, saved_out, out_grad, value_up):
    n_dp, n_head = mesh.shape["dp"], mesh.shape["head"]
    _, slots, heads, width = queries.shape
    latent = saved_out.shape[3]
    vhead = out_grad.shape[3]
    share = latent // (n_dp * 2)
    unit = 16 * n_head
    piece = -(-width // unit) * 16
    dims = (n_dp, n_head, heads, slots, width, latent, share)
    dma = pltpu.SemaphoreType.DMA
    chunks, steps = heads // PER_CHUNK, heads // PER_STEP
    results = pl.pallas_call(
        functools.partial(kernel, dims),
        out_shape=(
            jax.ShapeDtypeStruct((heads, width, slots), BF16),
            jax.ShapeDtypeStruct((width, slots), F32),
            jax.ShapeDtypeStruct((heads, share, vhead), F32),
        ),
        in_specs=[pl.BlockSpec(memory_space=pltpu.HBM)] * 7,
        out_specs=(pl.BlockSpec(memory_space=pl.ANY),) * 3,
        scratch_shapes=[
            pltpu.VMEM((heads, width, slots), BF16),
            pltpu.VMEM((2, width, slots), BF16),
            pltpu.VMEM((2, 1, slots), jnp.int32),
            pltpu.VMEM((heads, slots), F32),
            pltpu.VMEM((slots * heads, latent), BF16),
            pltpu.VMEM((slots * heads, vhead), BF16),
            pltpu.VMEM((heads, latent, vhead), BF16),
            pltpu.VMEM((slots * heads, 128), F32),
            pltpu.VMEM((slots * heads, 128), F32),
            pltpu.VMEM((slots * heads, vhead), F32),
            pltpu.VMEM((heads, slots, latent), BF16),
            pltpu.VMEM((heads, slots, vhead), BF16),
            pltpu.VMEM((steps, latent, PER_STEP * slots), BF16),
            pltpu.VMEM((steps, 1, PER_STEP * slots), F32),
            pltpu.VMEM((steps, 2 * slots, PER_STEP * slots), BF16),
            pltpu.VMEM((2 * slots, width), BF16),
            pltpu.VMEM((width, 2 * slots), BF16),
            pltpu.VMEM((2 * slots, slots), F32),
            pltpu.VMEM((2, heads, n_dp, share, vhead), BF16),
            pltpu.VMEM((heads, n_dp, share, vhead), BF16),
            pltpu.VMEM((n_dp, heads, share, vhead), BF16),
            pltpu.VMEM((n_dp, heads, share, vhead), BF16),
            pltpu.VMEM((piece * n_head, 2 * slots), F32),
            pltpu.VMEM((n_head, 2, piece, slots), BF16),
            pltpu.VMEM((n_head, 2, piece, slots), BF16),
            pltpu.VMEM((2, piece, slots), BF16),
            pltpu.VMEM((piece, slots), BF16),
            pltpu.VMEM((n_head, piece, slots), BF16),
            pltpu.VMEM((heads, width, slots), BF16),
            pltpu.VMEM((width, slots), F32),
            pltpu.VMEM((heads, share, vhead), F32),
            dma((7,)),
            dma((2,)), dma((2,)),
            dma((chunks,)), dma((chunks,)),
            dma((n_dp, chunks)), dma((n_dp, chunks)),
            dma((n_head,)), dma((n_head,)),
            dma((2,)),
            dma((n_head,)), dma((n_head,)),
            dma((2,)), dma((chunks,)),
        ],
        compiler_params=pltpu.CompilerParams(
            collective_id=0, has_side_effects=True, vmem_limit_bytes=64 * 1024 * 1024),
    )(
        jnp.transpose(queries[0], (1, 2, 0)),
        latents[0].T,
        positions,
        lse[0].T,
        saved_out.reshape(slots * heads, latent),
        out_grad.reshape(slots * heads, vhead),
        value_up,
    )
    query_grad, latent_grad, up_grad = pl.pallas_call(
        write_out,
        out_shape=(
            jax.ShapeDtypeStruct((heads, width, slots), BF16),
            jax.ShapeDtypeStruct((width, slots), F32),
            jax.ShapeDtypeStruct((share * heads, vhead), F32),
        ),
        in_specs=[pl.BlockSpec(memory_space=pl.ANY)] * 3,
        out_specs=(pl.BlockSpec(memory_space=pl.ANY),) * 3,
        scratch_shapes=[pltpu.VMEM(r.shape, r.dtype) for r in results] + [
            pltpu.VMEM((share * heads, vhead), F32), dma((6,)), dma((6,))],
        compiler_params=pltpu.CompilerParams(vmem_limit_bytes=64 * 1024 * 1024),
    )(*results)
    return (
        jnp.transpose(query_grad, (2, 0, 1))[None],
        latent_grad.T[None],
        up_grad.reshape(share, heads, vhead),
    )


def spans(length):
    return [(lower, min(length, lower + 512)) for lower in range(0, length, 512)]


def spread(queries, latents, positions, lse, saved_out, out_grad, value_up):
    query_rows = queries[0]
    slot_count = query_rows.shape[0]
    head_count = query_rows.shape[1]
    full_width = query_rows.shape[2]
    latent_width = saved_out.shape[3]
    query_pos = positions[0]
    row_lse = lse[0]
    latest = jnp.max(query_pos)
    scaling = (VHEAD + ROPE) ** (-0.5)
    lat_grad = jnp.einsum(
        "thv,hlv->thl", out_grad[0], value_up, preferred_element_type=jnp.float32
    ).astype(jnp.bfloat16)
    row_delta = jnp.sum(lat_grad.astype(jnp.float32) * saved_out[0].astype(jnp.float32), axis=-1)
    slab_rows = slot_count * lax.axis_size("ctx")
    carry = (
        jnp.zeros((slot_count, head_count, full_width), jnp.float32),
        jnp.zeros((slab_rows, full_width), jnp.float32),
    )
    keys_in = lax.all_gather(latents[0], "ctx", axis=0, tiled=True)
    pos_in = lax.all_gather(positions[0], "ctx", axis=0, tiled=True)
    for lower, upper in spans(keys_in.shape[0]):
        key_rows = keys_in[lower:upper]
        key_pos = pos_in[lower:upper]

        def update(state):
            query_acc, key_acc = state
            logits = (
                jnp.einsum("thd,kd->thk", query_rows, key_rows, preferred_element_type=jnp.float32)
                * scaling
            )
            visible = key_pos[None, None, :] <= query_pos[:, None, None]
            weights = jnp.where(visible, jnp.exp(logits - row_lse[:, :, None]), 0.0)
            dot_value = jnp.einsum(
                "thl,kl->thk",
                lat_grad,
                key_rows[:, :latent_width],
                preferred_element_type=jnp.float32,
            )
            dlogits = (weights * (dot_value - row_delta[:, :, None]) * scaling).astype(jnp.bfloat16)
            query_acc = query_acc + jnp.einsum(
                "thk,kd->thd", dlogits, key_rows, preferred_element_type=jnp.float32
            )
            key_term = jnp.einsum(
                "thk,thd->kd", dlogits, query_rows, preferred_element_type=jnp.float32
            )
            value_term = jnp.einsum(
                "thk,thl->kl",
                weights.astype(jnp.bfloat16),
                lat_grad,
                preferred_element_type=jnp.float32,
            )
            key_term = key_term + jnp.pad(value_term, ((0, 0), (0, full_width - latent_width)))
            previous = lax.dynamic_slice_in_dim(key_acc, 0 + lower, upper - lower, 0)
            key_acc = lax.dynamic_update_slice_in_dim(key_acc, previous + key_term, 0 + lower, 0)
            return (query_acc, key_acc)

        carry = lax.cond(jnp.min(key_pos) > latest, lambda state: state, update, carry)
    query_acc, key_acc = carry
    summed = lax.psum(key_acc, "head")
    own_rows = lax.psum_scatter(summed, "ctx", scatter_dimension=0, tiled=True)
    weight_share = lax.psum_scatter(
        jnp.einsum("thl,thv->lhv", saved_out[0], out_grad[0], preferred_element_type=jnp.float32),
        ("dp", "ctx"),
        scatter_dimension=0,
        tiled=True,
    )
    return (query_acc.astype(jnp.bfloat16)[None], own_rows[None], weight_share)


def solution(mesh):
    body = functools.partial(fused, mesh) if mesh.shape["ctx"] == 2 else spread
    return jax.shard_map(
        body,
        mesh=mesh,
        in_specs=(
            P("dp", "ctx", "head", None),
            P("dp", "ctx", None),
            P("dp", "ctx"),
            P("dp", "ctx", "head"),
            P("dp", "ctx", "head", None),
            P("dp", "ctx", "head", None),
            P("head", None, None),
        ),
        out_specs=(
            P("dp", "ctx", "head", None),
            P("dp", "ctx", None),
            P(("dp", "ctx"), "head", None),
        ),
        check_vma=False,
    )
```

```python
import functools

import jax
import jax.numpy as jnp
from jax import lax
from jax.experimental import pallas as pl
from jax.experimental.pallas import tpu as pltpu
from jax.sharding import PartitionSpec as P

ROPE = 32
VHEAD = 128
MESH = pl.DeviceIdType.MESH
BF16 = jnp.bfloat16
F32 = jnp.float32
PER_CHUNK = 4


def dot(lhs, rhs, over):
    return lax.dot_general(lhs, rhs, (((over[0],), (over[1],)), ((), ())), preferred_element_type=F32)


def slab_peers(my_ctx, my_head, n_head):
    ahead = [{"ctx": my_ctx, "head": lax.rem(my_head + step, n_head)} for step in range(1, n_head)]
    across = [{"ctx": 1 - my_ctx, "head": lax.rem(my_head + step, n_head)} for step in range(n_head)]
    return across + ahead


def kernel(
    dims,
    q_hbm, lat_hbm, pos_hbm, lse_hbm, saved_hbm, grad_hbm, up_hbm,
    qg_hbm, lg_hbm, vg_hbm,
    q_ref, kt_in, pos_in, lse_ref, saved_b, grad_b, up_ref,
    saved_lo, saved_hi, grad_f, lat_grads, deltas, dlogits_all,
    keys, keys_t, bias,
    vx, vr, zs, zr,
    key_acc, ka_send, ka_recv, kc,
    qg_ref, lg_ref, vg_ref,
    in_sem, lat_send, lat_recv, x_send, x_recv, z_send, z_recv,
    ka_ssem, ka_rsem, kc_ssem, kc_rsem, out_sem, vg_sem,
):
    n_dp, n_head, heads, slots, width, latent, share = dims
    scaling = (VHEAD + ROPE) ** -0.5
    my_dp, my_ctx, my_head = lax.axis_index("dp"), lax.axis_index("ctx"), lax.axis_index("head")
    other = 1 - my_ctx
    chunks = heads // PER_CHUNK
    piece = key_acc.shape[0] // n_head

    def load(index, source, target):
        copy = pltpu.make_async_copy(source, target, in_sem.at[index])
        copy.start()
        return copy

    lat_in = load(0, lat_hbm, kt_in.at[my_ctx])
    pos_load = load(1, pos_hbm, pos_in.at[my_ctx])
    saved_in = load(2, saved_hbm, saved_b)
    grad_in = load(3, grad_hbm, grad_b)

    barrier = pltpu.get_barrier_semaphore()
    for step in range(1, n_dp):
        pl.semaphore_signal(barrier, inc=1, device_id={"dp": lax.rem(my_dp + step, n_dp)}, device_id_type=MESH)
    peers = slab_peers(my_ctx, my_head, n_head)
    for where in peers:
        pl.semaphore_signal(barrier, inc=1, device_id=where, device_id_type=MESH)

    def send(source, target, send_sem, recv_sem, where):
        return pltpu.make_async_remote_copy(
            src_ref=source, dst_ref=target, send_sem=send_sem, recv_sem=recv_sem,
            device_id=where, device_id_type=MESH)

    saved_in.wait()
    grad_in.wait()
    up_in = load(4, up_hbm, up_ref)
    q_in = load(5, q_hbm, q_ref)
    lse_in = load(6, lse_hbm, lse_ref)
    rows_step = (slots * heads) // 8

    def widen(step, carry):
        rows = pl.ds(pl.multiple_of(step * rows_step, rows_step), rows_step)
        saved_lo[rows, :] = saved_b[rows, :128].astype(F32)
        saved_hi[rows, :] = saved_b[rows, 128:].astype(F32)
        grad_f[rows, :] = grad_b[rows, :].astype(F32)
        return carry

    lax.fori_loop(0, 8, widen, 0)

    lat_in.wait()
    pos_load.wait()
    pl.semaphore_wait(barrier, (n_dp - 1) + (2 * n_head - 1))
    lat_copy = send(kt_in.at[my_ctx], kt_in.at[my_ctx], lat_send.at[0], lat_recv.at[0], {"ctx": other})
    pos_copy = send(pos_in.at[my_ctx], pos_in.at[my_ctx], lat_send.at[1], lat_recv.at[1], {"ctx": other})
    lat_copy.start()
    pos_copy.start()

    def x_copy(chunk):
        part = pl.ds(chunk * PER_CHUNK, PER_CHUNK)
        return send(vx.at[other, part], vr.at[part], x_send.at[chunk], x_recv.at[chunk], {"ctx": other})

    diagonal = lax.broadcasted_iota(jnp.int32, (slots, slots), 0) == lax.broadcasted_iota(
        jnp.int32, (slots, slots), 1)
    up_in.wait()

    def up_partial(chunk, carry):
        members = [chunk * PER_CHUNK + offset for offset in range(PER_CHUNK)]
        lows, highs, grads = [], [], []
        for head in members:
            rows = pl.ds(head, slots, heads)
            lows.append(saved_lo[rows, :].astype(BF16))
            highs.append(saved_hi[rows, :].astype(BF16))
            grads.append(grad_f[rows, :].astype(BF16))
        for head, low, high, grad in zip(members, lows, highs, grads):
            product = jnp.concatenate([dot(low, grad, (0, 0)), dot(high, grad, (0, 0))], axis=0).astype(BF16)
            for dp in range(n_dp):
                for ctx in range(2):
                    first = (dp * 2 + ctx) * share
                    vx[ctx, head, dp] = product[first:first + share]
        x_copy(chunk).start()
        raised = [dot(up_ref[head], grad, (1, 1)).astype(BF16) for head, grad in zip(members, grads)]
        lat_grads[chunk] = jnp.concatenate(raised, axis=1)
        sums = []
        for low, high, lat_grad in zip(lows, highs, raised):
            full = dot(jnp.concatenate([low, high], axis=1), lat_grad, (1, 0))
            sums.append(jnp.sum(jnp.where(diagonal, full, 0.0), axis=0, keepdims=True))
        deltas[chunk] = jnp.concatenate(sums, axis=1)
        return carry

    lax.fori_loop(0, chunks, up_partial, 0)

    lat_copy.wait_recv()
    pos_copy.wait_recv()
    query_pos = pos_in[my_ctx]
    for half in range(2):
        cols = slice(half * slots, (half + 1) * slots)
        block = kt_in[half]
        keys_t[:, cols] = block
        keys[cols, :] = block.astype(F32).T.astype(BF16)
        key_pos = jnp.broadcast_to(pos_in[half], (slots, slots)).T
        bias[cols, :] = jnp.where(key_pos <= query_pos, 0.0, -1e30)
    key_acc[...] = jnp.zeros_like(key_acc)
    q_in.wait()
    lse_in.wait()

    def attend(chunk):
        members = [chunk * PER_CHUNK + offset for offset in range(PER_CHUNK)]
        query = jnp.concatenate([q_ref[head] for head in members], axis=1)
        lse = jnp.concatenate([lse_ref[pl.ds(head, 1), :] for head in members], axis=1)
        mask = jnp.concatenate([bias[...]] * PER_CHUNK, axis=1)
        lat_grad = lat_grads[chunk]
        logits = dot(keys[...], query, (1, 0)) * scaling
        dot_value = dot(keys[:, :latent], lat_grad, (1, 0))
        weights = jnp.exp(logits - lse + mask)
        dlogits = (weights * (dot_value - deltas[chunk]) * scaling).astype(BF16)
        dlogits_all[chunk] = dlogits
        key_term = dot(query, dlogits, (1, 1))
        value_term = dot(lat_grad, weights.astype(BF16), (1, 1))
        key_acc[:latent, :] += key_term[:latent] + value_term
        key_acc[latent:width, :] += key_term[latent:]

    def z_copy(step, chunk, arriving=False):
        peer = lax.rem(my_dp + step, n_dp)
        part = pl.ds(chunk * PER_CHUNK, PER_CHUNK)
        slot = peer if arriving else my_dp
        return send(zs.at[peer, part], zr.at[slot, part], z_send.at[peer, chunk], z_recv.at[slot, chunk], {"dp": peer})

    def forward(chunk):
        x_copy(chunk).wait_recv()
        for offset in range(PER_CHUNK):
            head = chunk * PER_CHUNK + offset
            for dp in range(n_dp):
                zs[dp, head] = (vx[my_ctx, head, dp].astype(F32) + vr[head, dp].astype(F32)).astype(BF16)
        for step in range(1, n_dp):
            z_copy(step, chunk).start()

    def attend_and_forward(chunk, carry):
        attend(chunk)

        @pl.when(chunk == 1)
        def _():
            forward(0)

        return carry

    lax.fori_loop(0, chunks, attend_and_forward, 0)

    for ctx in range(2):
        for part in range(n_head):
            ka_send[ctx, part] = key_acc[
                part * piece:(part + 1) * piece, ctx * slots:(ctx + 1) * slots].astype(BF16)

    def ka_copy(where, arriving=False):
        theirs, mine = (where["ctx"], where["head"]), (my_ctx, my_head)
        slot = theirs if arriving else mine
        return send(ka_send.at[theirs], ka_recv.at[slot], ka_ssem.at[theirs], ka_rsem.at[slot], where)

    for where in peers:
        ka_copy(where).start()

    forward(1)

    def query_grads(chunk, carry):
        query_grad = dot(keys_t[...], dlogits_all[chunk], (1, 0)).astype(BF16)
        for offset in range(PER_CHUNK):
            qg_ref[chunk * PER_CHUNK + offset] = query_grad[:, offset * slots:(offset + 1) * slots]
        return carry

    lax.fori_loop(0, chunks, query_grads, 0)
    qg_copy = pltpu.make_async_copy(qg_ref, qg_hbm, out_sem.at[0])
    qg_copy.start()

    sums = ka_send[my_ctx, my_head].astype(F32)
    for where in peers:
        ka_copy(where, arriving=True).wait_recv()
        sums = sums + ka_recv[where["ctx"], where["head"]].astype(F32)
    kc[my_head] = sums.astype(BF16)
    kc_copies = []
    for step in range(1, n_head):
        to = lax.rem(my_head + step, n_head)
        copy = send(kc.at[my_head], kc.at[my_head], kc_ssem.at[to], kc_rsem.at[my_head], {"head": to})
        copy.start()
        kc_copies.append(copy)

    for chunk in range(2, chunks):
        forward(chunk)

    def vg_copy(chunk):
        part = pl.ds(chunk * PER_CHUNK, PER_CHUNK)
        return pltpu.make_async_copy(vg_ref.at[part], vg_hbm.at[part], vg_sem.at[chunk])

    def finish(chunk, carry):
        for step in range(1, n_dp):
            z_copy(step, chunk, arriving=True).wait_recv()
        for offset in range(PER_CHUNK):
            head = chunk * PER_CHUNK + offset
            total = zs[my_dp, head].astype(F32)
            for step in range(1, n_dp):
                total = total + zr[lax.rem(my_dp + step, n_dp), head].astype(F32)
            vg_ref[head] = total
        vg_copy(chunk).start()
        return carry

    lax.fori_loop(0, chunks - 1, finish, 0)
    for step in range(1, n_head):
        src = lax.rem(my_head + step, n_head)
        send(kc.at[src], kc.at[src], kc_ssem.at[src], kc_rsem.at[src], {"head": src}).wait_recv()
    for part in range(n_head):
        first, last = part * piece, min((part + 1) * piece, width)
        lg_ref[first:last, :] = kc[part, :last - first, :].astype(F32)
    lg_copy = pltpu.make_async_copy(lg_ref, lg_hbm, out_sem.at[1])
    lg_copy.start()
    lax.fori_loop(chunks - 1, chunks, finish, 0)

    def drain(chunk, carry):
        x_copy(chunk).wait_send()
        for step in range(1, n_dp):
            z_copy(step, chunk).wait_send()
        vg_copy(chunk).wait()
        return carry

    lax.fori_loop(0, chunks, drain, 0)
    for copy in [lat_copy, pos_copy] + [ka_copy(where) for where in peers] + kc_copies:
        copy.wait_send()
    qg_copy.wait()
    lg_copy.wait()


def write_out(qg_hbm, lg_hbm, vg_hbm, qg_out, lg_out, vg_out, qg_ref, lg_ref, vg_ref, vg_rows, in_sem, out_sem):
    heads, share, _ = vg_ref.shape
    come = pltpu.make_async_copy(vg_hbm, vg_ref, in_sem.at[0])
    leave = pltpu.make_async_copy(vg_rows, vg_out, out_sem.at[0])
    pieces = [(
        pltpu.make_async_copy(lg_hbm, lg_ref, in_sem.at[1]),
        pltpu.make_async_copy(lg_ref, lg_out, out_sem.at[1]))]
    size = heads // 4
    for part in range(4):
        rows = pl.ds(part * size, size)
        pieces.append((
            pltpu.make_async_copy(qg_hbm.at[rows], qg_ref.at[rows], in_sem.at[2 + part]),
            pltpu.make_async_copy(qg_ref.at[rows], qg_out.at[rows], out_sem.at[2 + part])))
    come.start()
    for first, _ in pieces:
        first.start()
    come.wait()
    for head in range(heads):
        vg_rows[pl.ds(head, share, heads), :] = vg_ref[head]
    leave.start()
    for first, second in pieces:
        first.wait()
        second.start()
    leave.wait()
    for _, second in pieces:
        second.wait()


def fused(mesh, queries, latents, positions, lse, saved_out, out_grad, value_up):
    n_dp, n_head = mesh.shape["dp"], mesh.shape["head"]
    _, slots, heads, width = queries.shape
    latent = saved_out.shape[3]
    vhead = out_grad.shape[3]
    share = latent // (n_dp * 2)
    unit = 16 * n_head
    piece = -(-width // unit) * 16
    dims = (n_dp, n_head, heads, slots, width, latent, share)
    dma = pltpu.SemaphoreType.DMA
    chunks = heads // PER_CHUNK
    results = pl.pallas_call(
        functools.partial(kernel, dims),
        out_shape=(
            jax.ShapeDtypeStruct((heads, width, slots), BF16),
            jax.ShapeDtypeStruct((width, slots), F32),
            jax.ShapeDtypeStruct((heads, share, vhead), F32),
        ),
        in_specs=[pl.BlockSpec(memory_space=pltpu.HBM)] * 7,
        out_specs=(pl.BlockSpec(memory_space=pl.ANY),) * 3,
        scratch_shapes=[
            pltpu.VMEM((heads, width, slots), BF16),
            pltpu.VMEM((2, width, slots), BF16),
            pltpu.VMEM((2, 1, slots), jnp.int32),
            pltpu.VMEM((heads, slots), F32),
            pltpu.VMEM((slots * heads, latent), BF16),
            pltpu.VMEM((slots * heads, vhead), BF16),
            pltpu.VMEM((heads, latent, vhead), BF16),
            pltpu.VMEM((slots * heads, 128), F32),
            pltpu.VMEM((slots * heads, 128), F32),
            pltpu.VMEM((slots * heads, vhead), F32),
            pltpu.VMEM((chunks, latent, PER_CHUNK * slots), BF16),
            pltpu.VMEM((chunks, 1, PER_CHUNK * slots), F32),
            pltpu.VMEM((chunks, 2 * slots, PER_CHUNK * slots), BF16),
            pltpu.VMEM((2 * slots, width), BF16),
            pltpu.VMEM((width, 2 * slots), BF16),
            pltpu.VMEM((2 * slots, slots), F32),
            pltpu.VMEM((2, heads, n_dp, share, vhead), BF16),
            pltpu.VMEM((heads, n_dp, share, vhead), BF16),
            pltpu.VMEM((n_dp, heads, share, vhead), BF16),
            pltpu.VMEM((n_dp, heads, share, vhead), BF16),
            pltpu.VMEM((piece * n_head, 2 * slots), F32),
            pltpu.VMEM((2, n_head, piece, slots), BF16),
            pltpu.VMEM((2, n_head, piece, slots), BF16),
            pltpu.VMEM((n_head, piece, slots), BF16),
            pltpu.VMEM((heads, width, slots), BF16),
            pltpu.VMEM((width, slots), F32),
            pltpu.VMEM((heads, share, vhead), F32),
            dma((7,)),
            dma((2,)), dma((2,)),
            dma((chunks,)), dma((chunks,)),
            dma((n_dp, chunks)), dma((n_dp, chunks)),
            dma((2, n_head)), dma((2, n_head)),
            dma((n_head,)), dma((n_head,)),
            dma((2,)), dma((chunks,)),
        ],
        compiler_params=pltpu.CompilerParams(
            collective_id=0, has_side_effects=True, vmem_limit_bytes=64 * 1024 * 1024),
    )(
        jnp.transpose(queries[0], (1, 2, 0)),
        latents[0].T,
        positions,
        lse[0].T,
        saved_out.reshape(slots * heads, latent),
        out_grad.reshape(slots * heads, vhead),
        value_up,
    )
    query_grad, latent_grad, up_grad = pl.pallas_call(
        write_out,
        out_shape=(
            jax.ShapeDtypeStruct((heads, width, slots), BF16),
            jax.ShapeDtypeStruct((width, slots), F32),
            jax.ShapeDtypeStruct((share * heads, vhead), F32),
        ),
        in_specs=[pl.BlockSpec(memory_space=pl.ANY)] * 3,
        out_specs=(pl.BlockSpec(memory_space=pl.ANY),) * 3,
        scratch_shapes=[pltpu.VMEM(r.shape, r.dtype) for r in results] + [
            pltpu.VMEM((share * heads, vhead), F32), dma((6,)), dma((6,))],
        compiler_params=pltpu.CompilerParams(vmem_limit_bytes=64 * 1024 * 1024),
    )(*results)
    return (
        jnp.transpose(query_grad, (2, 0, 1))[None],
        latent_grad.T[None],
        up_grad.reshape(share, heads, vhead),
    )


def spans(length):
    return [(lower, min(length, lower + 512)) for lower in range(0, length, 512)]


def spread(queries, latents, positions, lse, saved_out, out_grad, value_up):
    query_rows = queries[0]
    slot_count = query_rows.shape[0]
    head_count = query_rows.shape[1]
    full_width = query_rows.shape[2]
    latent_width = saved_out.shape[3]
    query_pos = positions[0]
    row_lse = lse[0]
    latest = jnp.max(query_pos)
    scaling = (VHEAD + ROPE) ** (-0.5)
    lat_grad = jnp.einsum(
        "thv,hlv->thl", out_grad[0], value_up, preferred_element_type=jnp.float32
    ).astype(jnp.bfloat16)
    row_delta = jnp.sum(lat_grad.astype(jnp.float32) * saved_out[0].astype(jnp.float32), axis=-1)
    slab_rows = slot_count * lax.axis_size("ctx")
    carry = (
        jnp.zeros((slot_count, head_count, full_width), jnp.float32),
        jnp.zeros((slab_rows, full_width), jnp.float32),
    )
    keys_in = lax.all_gather(latents[0], "ctx", axis=0, tiled=True)
    pos_in = lax.all_gather(positions[0], "ctx", axis=0, tiled=True)
    for lower, upper in spans(keys_in.shape[0]):
        key_rows = keys_in[lower:upper]
        key_pos = pos_in[lower:upper]

        def update(state):
            query_acc, key_acc = state
            logits = (
                jnp.einsum("thd,kd->thk", query_rows, key_rows, preferred_element_type=jnp.float32)
                * scaling
            )
            visible = key_pos[None, None, :] <= query_pos[:, None, None]
            weights = jnp.where(visible, jnp.exp(logits - row_lse[:, :, None]), 0.0)
            dot_value = jnp.einsum(
                "thl,kl->thk",
                lat_grad,
                key_rows[:, :latent_width],
                preferred_element_type=jnp.float32,
            )
            dlogits = (weights * (dot_value - row_delta[:, :, None]) * scaling).astype(jnp.bfloat16)
            query_acc = query_acc + jnp.einsum(
                "thk,kd->thd", dlogits, key_rows, preferred_element_type=jnp.float32
            )
            key_term = jnp.einsum(
                "thk,thd->kd", dlogits, query_rows, preferred_element_type=jnp.float32
            )
            value_term = jnp.einsum(
                "thk,thl->kl",
                weights.astype(jnp.bfloat16),
                lat_grad,
                preferred_element_type=jnp.float32,
            )
            key_term = key_term + jnp.pad(value_term, ((0, 0), (0, full_width - latent_width)))
            previous = lax.dynamic_slice_in_dim(key_acc, 0 + lower, upper - lower, 0)
            key_acc = lax.dynamic_update_slice_in_dim(key_acc, previous + key_term, 0 + lower, 0)
            return (query_acc, key_acc)

        carry = lax.cond(jnp.min(key_pos) > latest, lambda state: state, update, carry)
    query_acc, key_acc = carry
    summed = lax.psum(key_acc, "head")
    own_rows = lax.psum_scatter(summed, "ctx", scatter_dimension=0, tiled=True)
    weight_share = lax.psum_scatter(
        jnp.einsum("thl,thv->lhv", saved_out[0], out_grad[0], preferred_element_type=jnp.float32),
        ("dp", "ctx"),
        scatter_dimension=0,
        tiled=True,
    )
    return (query_acc.astype(jnp.bfloat16)[None], own_rows[None], weight_share)


def solution(mesh):
    body = functools.partial(fused, mesh) if mesh.shape["ctx"] == 2 else spread
    return jax.shard_map(
        body,
        mesh=mesh,
        in_specs=(
            P("dp", "ctx", "head", None),
            P("dp", "ctx", None),
            P("dp", "ctx"),
            P("dp", "ctx", "head"),
            P("dp", "ctx", "head", None),
            P("dp", "ctx", "head", None),
            P("head", None, None),
        ),
        out_specs=(
            P("dp", "ctx", "head", None),
            P("dp", "ctx", None),
            P(("dp", "ctx"), "head", None),
        ),
        check_vma=False,
    )
```

```python
import functools

import jax
import jax.numpy as jnp
from jax import lax
from jax.experimental import pallas as pl
from jax.experimental.pallas import tpu as pltpu
from jax.sharding import PartitionSpec as P

ROPE = 32
VHEAD = 128
MESH = pl.DeviceIdType.MESH
BF16 = jnp.bfloat16
F32 = jnp.float32
PER_CHUNK = 4


def dot(lhs, rhs, over):
    return lax.dot_general(lhs, rhs, (((over[0],), (over[1],)), ((), ())), preferred_element_type=F32)


def slab_peers(my_ctx, my_head, n_head):
    ahead = [{"ctx": my_ctx, "head": lax.rem(my_head + step, n_head)} for step in range(1, n_head)]
    across = [{"ctx": 1 - my_ctx, "head": lax.rem(my_head + step, n_head)} for step in range(n_head)]
    return across + ahead


def kernel(
    dims,
    q_hbm, lat_hbm, pos_hbm, lse_hbm, saved_hbm, grad_hbm, up_hbm,
    qg_hbm, lg_out, vg_out,
    q_ref, kt_in, pos_in, lse_ref, saved_b, grad_b, up_ref,
    saved_lo, saved_hi, grad_f, lat_grads, deltas, dlogits_all,
    keys, keys_t, bias,
    vx, vr, zs, zr,
    key_acc, ka_send, ka_recv, kc,
    qg_ref,
    in_sem, lat_send, lat_recv, x_send, x_recv, z_send, z_recv,
    ka_ssem, ka_rsem, kc_ssem, kc_rsem, out_sem,
):
    n_dp, n_head, heads, slots, width, latent, share = dims
    scaling = (VHEAD + ROPE) ** -0.5
    my_dp, my_ctx, my_head = lax.axis_index("dp"), lax.axis_index("ctx"), lax.axis_index("head")
    other = 1 - my_ctx
    chunks = heads // PER_CHUNK
    piece = key_acc.shape[0] // n_head

    def load(index, source, target):
        copy = pltpu.make_async_copy(source, target, in_sem.at[index])
        copy.start()
        return copy

    lat_in = load(0, lat_hbm, kt_in.at[my_ctx])
    pos_load = load(1, pos_hbm, pos_in.at[my_ctx])
    saved_in = load(2, saved_hbm, saved_b)
    grad_in = load(3, grad_hbm, grad_b)
    up_in = load(4, up_hbm, up_ref)
    q_in = load(5, q_hbm, q_ref)
    lse_in = load(6, lse_hbm, lse_ref)

    barrier = pltpu.get_barrier_semaphore()
    for step in range(1, n_dp):
        pl.semaphore_signal(barrier, inc=1, device_id={"dp": lax.rem(my_dp + step, n_dp)}, device_id_type=MESH)
    for where in slab_peers(my_ctx, my_head, n_head):
        pl.semaphore_signal(barrier, inc=1, device_id=where, device_id_type=MESH)
    lat_in.wait()
    pos_load.wait()
    pl.semaphore_wait(barrier, (n_dp - 1) + (2 * n_head - 1))

    def send(source, target, send_sem, recv_sem, where):
        return pltpu.make_async_remote_copy(
            src_ref=source, dst_ref=target, send_sem=send_sem, recv_sem=recv_sem,
            device_id=where, device_id_type=MESH)

    lat_copy = send(kt_in.at[my_ctx], kt_in.at[my_ctx], lat_send.at[0], lat_recv.at[0], {"ctx": other})
    pos_copy = send(pos_in.at[my_ctx], pos_in.at[my_ctx], lat_send.at[1], lat_recv.at[1], {"ctx": other})
    lat_copy.start()
    pos_copy.start()

    saved_in.wait()
    grad_in.wait()
    rows_step = (slots * heads) // 8

    def widen(step, carry):
        rows = pl.ds(pl.multiple_of(step * rows_step, rows_step), rows_step)
        saved_lo[rows, :] = saved_b[rows, :128].astype(F32)
        saved_hi[rows, :] = saved_b[rows, 128:].astype(F32)
        grad_f[rows, :] = grad_b[rows, :].astype(F32)
        return carry

    lax.fori_loop(0, 8, widen, 0)

    def x_copy(chunk):
        part = pl.ds(chunk * PER_CHUNK, PER_CHUNK)
        return send(vx.at[other, part], vr.at[part], x_send.at[chunk], x_recv.at[chunk], {"ctx": other})

    diagonal = lax.broadcasted_iota(jnp.int32, (slots, slots), 0) == lax.broadcasted_iota(
        jnp.int32, (slots, slots), 1)
    up_in.wait()

    def up_partial(chunk, carry):
        members = [chunk * PER_CHUNK + offset for offset in range(PER_CHUNK)]
        lows, highs, grads = [], [], []
        for head in members:
            rows = pl.ds(head, slots, heads)
            lows.append(saved_lo[rows, :].astype(BF16))
            highs.append(saved_hi[rows, :].astype(BF16))
            grads.append(grad_f[rows, :].astype(BF16))
        for head, low, high, grad in zip(members, lows, highs, grads):
            product = jnp.concatenate([dot(low, grad, (0, 0)), dot(high, grad, (0, 0))], axis=0).astype(BF16)
            for dp in range(n_dp):
                for ctx in range(2):
                    first = (dp * 2 + ctx) * share
                    vx[ctx, head, dp] = product[first:first + share]
        x_copy(chunk).start()
        raised = [dot(up_ref[head], grad, (1, 1)).astype(BF16) for head, grad in zip(members, grads)]
        lat_grads[chunk] = jnp.concatenate(raised, axis=1)
        sums = []
        for low, high, lat_grad in zip(lows, highs, raised):
            full = dot(jnp.concatenate([low, high], axis=1), lat_grad, (1, 0))
            sums.append(jnp.sum(jnp.where(diagonal, full, 0.0), axis=0, keepdims=True))
        deltas[chunk] = jnp.concatenate(sums, axis=1)
        return carry

    lax.fori_loop(0, chunks, up_partial, 0)

    lat_copy.wait_recv()
    pos_copy.wait_recv()
    query_pos = pos_in[my_ctx]
    for half in range(2):
        cols = slice(half * slots, (half + 1) * slots)
        block = kt_in[half]
        keys_t[:, cols] = block
        keys[cols, :] = block.astype(F32).T.astype(BF16)
        key_pos = jnp.broadcast_to(pos_in[half], (slots, slots)).T
        bias[cols, :] = jnp.where(key_pos <= query_pos, 0.0, -1e30)
    key_acc[...] = jnp.zeros_like(key_acc)
    q_in.wait()
    lse_in.wait()

    def attend(chunk):
        members = [chunk * PER_CHUNK + offset for offset in range(PER_CHUNK)]
        query = jnp.concatenate([q_ref[head] for head in members], axis=1)
        lse = jnp.concatenate([lse_ref[pl.ds(head, 1), :] for head in members], axis=1)
        mask = jnp.concatenate([bias[...]] * PER_CHUNK, axis=1)
        lat_grad = lat_grads[chunk]
        logits = dot(keys[...], query, (1, 0)) * scaling
        dot_value = dot(keys[:, :latent], lat_grad, (1, 0))
        weights = jnp.exp(logits - lse + mask)
        dlogits = (weights * (dot_value - deltas[chunk]) * scaling).astype(BF16)
        dlogits_all[chunk] = dlogits
        key_term = dot(query, dlogits, (1, 1))
        value_term = dot(lat_grad, weights.astype(BF16), (1, 1))
        key_acc[:latent, :] += key_term[:latent] + value_term
        key_acc[latent:width, :] += key_term[latent:]

    near = my_dp + 1 - 2 * lax.rem(my_dp, 2)
    far = lax.rem(my_dp + 2, n_dp)

    def z_copy(slot, chunk):
        part = pl.ds(chunk * PER_CHUNK, PER_CHUNK)
        piece_at, to = ((near, near), (lax.rem(near + 2, n_dp), near), (far, far))[slot]
        return send(zs.at[piece_at, part], zr.at[slot, part], z_send.at[slot, chunk], z_recv.at[slot, chunk], {"dp": to})

    def forward(chunk):
        x_copy(chunk).wait_recv()
        for offset in range(PER_CHUNK):
            head = chunk * PER_CHUNK + offset
            for dp in range(n_dp):
                zs[dp, head] = (vx[my_ctx, head, dp].astype(F32) + vr[head, dp].astype(F32)).astype(BF16)
        z_copy(1, chunk).start()
        z_copy(0, chunk).start()

    def pass_on(chunk):
        z_copy(1, chunk).wait_recv()
        for offset in range(PER_CHUNK):
            head = chunk * PER_CHUNK + offset
            zs[far, head] = (zs[far, head].astype(F32) + zr[1, head].astype(F32)).astype(BF16)
        z_copy(2, chunk).start()

    def attend_and_forward(chunk, carry):
        attend(chunk)

        @pl.when(chunk < chunks - 1)
        def _():
            forward(chunk)

        @pl.when((chunk >= 1) & (chunk < chunks - 1))
        def _():
            pass_on(chunk - 1)

        return carry

    lax.fori_loop(0, chunks, attend_and_forward, 0)

    for ctx in range(2):
        for part in range(n_head):
            ka_send[ctx, part] = key_acc[
                part * piece:(part + 1) * piece, ctx * slots:(ctx + 1) * slots].astype(BF16)

    def ka_copy(where, arriving=False):
        theirs, mine = (where["ctx"], where["head"]), (my_ctx, my_head)
        slot = theirs if arriving else mine
        return send(ka_send.at[theirs], ka_recv.at[slot], ka_ssem.at[theirs], ka_rsem.at[slot], where)

    peers = slab_peers(my_ctx, my_head, n_head)
    for where in peers:
        ka_copy(where).start()

    forward(chunks - 1)
    pass_on(chunks - 2)

    def query_grads(chunk, carry):
        query_grad = dot(keys_t[...], dlogits_all[chunk], (1, 0)).astype(BF16)
        for offset in range(PER_CHUNK):
            qg_ref[chunk * PER_CHUNK + offset] = query_grad[:, offset * slots:(offset + 1) * slots]
        return carry

    lax.fori_loop(0, chunks, query_grads, 0)
    qg_copy = pltpu.make_async_copy(qg_ref, qg_hbm, out_sem)
    qg_copy.start()

    sums = ka_send[my_ctx, my_head].astype(F32)
    for where in peers:
        ka_copy(where, arriving=True).wait_recv()
        sums = sums + ka_recv[where["ctx"], where["head"]].astype(F32)
    kc[my_head] = sums.astype(BF16)
    kc_copies = []
    for step in range(1, n_head):
        to = lax.rem(my_head + step, n_head)
        copy = send(kc.at[my_head], kc.at[my_head], kc_ssem.at[to], kc_rsem.at[my_head], {"head": to})
        copy.start()
        kc_copies.append(copy)

    pass_on(chunks - 1)

    def finish(chunk, carry):
        z_copy(0, chunk).wait_recv()
        z_copy(2, chunk).wait_recv()
        for offset in range(PER_CHUNK):
            head = chunk * PER_CHUNK + offset
            total = zs[my_dp, head].astype(F32)
            total = total + zr[0, head].astype(F32) + zr[2, head].astype(F32)
            vg_out[pl.ds(head, share, heads), :] = total
        return carry

    lax.fori_loop(0, chunks, finish, 0)

    for step in range(1, n_head):
        src = lax.rem(my_head + step, n_head)
        send(kc.at[src], kc.at[src], kc_ssem.at[src], kc_rsem.at[src], {"head": src}).wait_recv()
    for part in range(n_head):
        first, last = part * piece, min((part + 1) * piece, width)
        lg_out[first:last, :] = kc[part, :last - first, :].astype(F32)

    def drain(chunk, carry):
        x_copy(chunk).wait_send()
        for slot in range(3):
            z_copy(slot, chunk).wait_send()
        return carry

    lax.fori_loop(0, chunks, drain, 0)
    for copy in [lat_copy, pos_copy] + [ka_copy(where) for where in peers] + kc_copies:
        copy.wait_send()
    qg_copy.wait()


def write_out(*refs):
    sources, targets, rooms, (in_sem, out_sem) = refs[:3], refs[3:6], refs[6:9], refs[9:]
    pieces = []
    for source, target, room in zip(sources, targets, rooms):
        count = 4 if source.ndim == 3 else 1
        size = source.shape[0] // count
        for part in range(count):
            rows = pl.ds(part * size, size)
            index = len(pieces)
            pieces.append((
                pltpu.make_async_copy(source.at[rows], room.at[rows], in_sem.at[index]),
                pltpu.make_async_copy(room.at[rows], target.at[rows], out_sem.at[index])))
    for come, _ in pieces:
        come.start()
    for come, leave in pieces:
        come.wait()
        leave.start()
    for _, leave in pieces:
        leave.wait()


def fused(mesh, queries, latents, positions, lse, saved_out, out_grad, value_up):
    n_dp, n_head = mesh.shape["dp"], mesh.shape["head"]
    _, slots, heads, width = queries.shape
    latent = saved_out.shape[3]
    vhead = out_grad.shape[3]
    share = latent // (n_dp * 2)
    unit = 16 * n_head
    piece = -(-width // unit) * 16
    dims = (n_dp, n_head, heads, slots, width, latent, share)
    dma = pltpu.SemaphoreType.DMA
    chunks = heads // PER_CHUNK
    results = pl.pallas_call(
        functools.partial(kernel, dims),
        out_shape=(
            jax.ShapeDtypeStruct((heads, width, slots), BF16),
            jax.ShapeDtypeStruct((width, slots), F32),
            jax.ShapeDtypeStruct((share * heads, vhead), F32),
        ),
        in_specs=[pl.BlockSpec(memory_space=pltpu.HBM)] * 7,
        out_specs=(
            pl.BlockSpec(memory_space=pl.ANY),
            pl.BlockSpec(memory_space=pltpu.VMEM),
            pl.BlockSpec(memory_space=pltpu.VMEM),
        ),
        scratch_shapes=[
            pltpu.VMEM((heads, width, slots), BF16),
            pltpu.VMEM((2, width, slots), BF16),
            pltpu.VMEM((2, 1, slots), jnp.int32),
            pltpu.VMEM((heads, slots), F32),
            pltpu.VMEM((slots * heads, latent), BF16),
            pltpu.VMEM((slots * heads, vhead), BF16),
            pltpu.VMEM((heads, latent, vhead), BF16),
            pltpu.VMEM((slots * heads, 128), F32),
            pltpu.VMEM((slots * heads, 128), F32),
            pltpu.VMEM((slots * heads, vhead), F32),
            pltpu.VMEM((chunks, latent, PER_CHUNK * slots), BF16),
            pltpu.VMEM((chunks, 1, PER_CHUNK * slots), F32),
            pltpu.VMEM((chunks, 2 * slots, PER_CHUNK * slots), BF16),
            pltpu.VMEM((2 * slots, width), BF16),
            pltpu.VMEM((width, 2 * slots), BF16),
            pltpu.VMEM((2 * slots, slots), F32),
            pltpu.VMEM((2, heads, n_dp, share, vhead), BF16),
            pltpu.VMEM((heads, n_dp, share, vhead), BF16),
            pltpu.VMEM((n_dp, heads, share, vhead), BF16),
            pltpu.VMEM((n_dp, heads, share, vhead), BF16),
            pltpu.VMEM((piece * n_head, 2 * slots), F32),
            pltpu.VMEM((2, n_head, piece, slots), BF16),
            pltpu.VMEM((2, n_head, piece, slots), BF16),
            pltpu.VMEM((n_head, piece, slots), BF16),
            pltpu.VMEM((heads, width, slots), BF16),
            dma((7,)),
            dma((2,)), dma((2,)),
            dma((chunks,)), dma((chunks,)),
            dma((n_dp, chunks)), dma((n_dp, chunks)),
            dma((2, n_head)), dma((2, n_head)),
            dma((n_head,)), dma((n_head,)),
            dma,
        ],
        compiler_params=pltpu.CompilerParams(
            collective_id=0, has_side_effects=True, vmem_limit_bytes=64 * 1024 * 1024),
    )(
        jnp.transpose(queries[0], (1, 2, 0)),
        latents[0].T,
        positions,
        lse[0].T,
        saved_out.reshape(slots * heads, latent),
        out_grad.reshape(slots * heads, vhead),
        value_up,
    )
    query_grad, latent_grad, up_grad = pl.pallas_call(
        write_out,
        out_shape=tuple(jax.ShapeDtypeStruct(r.shape, r.dtype) for r in results),
        in_specs=[pl.BlockSpec(memory_space=pl.ANY)] * 3,
        out_specs=(pl.BlockSpec(memory_space=pl.ANY),) * 3,
        scratch_shapes=[pltpu.VMEM(r.shape, r.dtype) for r in results] + [dma((6,)), dma((6,))],
        compiler_params=pltpu.CompilerParams(vmem_limit_bytes=64 * 1024 * 1024),
    )(*results)
    return (
        jnp.transpose(query_grad, (2, 0, 1))[None],
        latent_grad.T[None],
        up_grad.reshape(share, heads, vhead),
    )


def spans(length):
    return [(lower, min(length, lower + 512)) for lower in range(0, length, 512)]


def spread(queries, latents, positions, lse, saved_out, out_grad, value_up):
    query_rows = queries[0]
    slot_count = query_rows.shape[0]
    head_count = query_rows.shape[1]
    full_width = query_rows.shape[2]
    latent_width = saved_out.shape[3]
    query_pos = positions[0]
    row_lse = lse[0]
    latest = jnp.max(query_pos)
    scaling = (VHEAD + ROPE) ** (-0.5)
    lat_grad = jnp.einsum(
        "thv,hlv->thl", out_grad[0], value_up, preferred_element_type=jnp.float32
    ).astype(jnp.bfloat16)
    row_delta = jnp.sum(lat_grad.astype(jnp.float32) * saved_out[0].astype(jnp.float32), axis=-1)
    slab_rows = slot_count * lax.axis_size("ctx")
    carry = (
        jnp.zeros((slot_count, head_count, full_width), jnp.float32),
        jnp.zeros((slab_rows, full_width), jnp.float32),
    )
    keys_in = lax.all_gather(latents[0], "ctx", axis=0, tiled=True)
    pos_in = lax.all_gather(positions[0], "ctx", axis=0, tiled=True)
    for lower, upper in spans(keys_in.shape[0]):
        key_rows = keys_in[lower:upper]
        key_pos = pos_in[lower:upper]

        def update(state):
            query_acc, key_acc = state
            logits = (
                jnp.einsum("thd,kd->thk", query_rows, key_rows, preferred_element_type=jnp.float32)
                * scaling
            )
            visible = key_pos[None, None, :] <= query_pos[:, None, None]
            weights = jnp.where(visible, jnp.exp(logits - row_lse[:, :, None]), 0.0)
            dot_value = jnp.einsum(
                "thl,kl->thk",
                lat_grad,
                key_rows[:, :latent_width],
                preferred_element_type=jnp.float32,
            )
            dlogits = (weights * (dot_value - row_delta[:, :, None]) * scaling).astype(jnp.bfloat16)
            query_acc = query_acc + jnp.einsum(
                "thk,kd->thd", dlogits, key_rows, preferred_element_type=jnp.float32
            )
            key_term = jnp.einsum(
                "thk,thd->kd", dlogits, query_rows, preferred_element_type=jnp.float32
            )
            value_term = jnp.einsum(
                "thk,thl->kl",
                weights.astype(jnp.bfloat16),
                lat_grad,
                preferred_element_type=jnp.float32,
            )
            key_term = key_term + jnp.pad(value_term, ((0, 0), (0, full_width - latent_width)))
            previous = lax.dynamic_slice_in_dim(key_acc, 0 + lower, upper - lower, 0)
            key_acc = lax.dynamic_update_slice_in_dim(key_acc, previous + key_term, 0 + lower, 0)
            return (query_acc, key_acc)

        carry = lax.cond(jnp.min(key_pos) > latest, lambda state: state, update, carry)
    query_acc, key_acc = carry
    summed = lax.psum(key_acc, "head")
    own_rows = lax.psum_scatter(summed, "ctx", scatter_dimension=0, tiled=True)
    weight_share = lax.psum_scatter(
        jnp.einsum("thl,thv->lhv", saved_out[0], out_grad[0], preferred_element_type=jnp.float32),
        ("dp", "ctx"),
        scatter_dimension=0,
        tiled=True,
    )
    return (query_acc.astype(jnp.bfloat16)[None], own_rows[None], weight_share)


def solution(mesh):
    body = functools.partial(fused, mesh) if (mesh.shape["ctx"], mesh.shape["dp"]) == (2, 4) else spread
    return jax.shard_map(
        body,
        mesh=mesh,
        in_specs=(
            P("dp", "ctx", "head", None),
            P("dp", "ctx", None),
            P("dp", "ctx"),
            P("dp", "ctx", "head"),
            P("dp", "ctx", "head", None),
            P("dp", "ctx", "head", None),
            P("head", None, None),
        ),
        out_specs=(
            P("dp", "ctx", "head", None),
            P("dp", "ctx", None),
            P(("dp", "ctx"), "head", None),
        ),
        check_vma=False,
    )
```
